32 devices in a mesh: grp: 2 (over x), facet: 16 (over z, y, core).
Axes of the slice: x: 2, y: 2, z: 4, core: 2. Of those that a mesh axis runs over, the one named last changes fastest.
Arguments:
- subgrids: bfloat16 [32, 2, 8192, 128], P(('grp', 'facet')), parts along dimension 0, may hold values from -6 to 6
- taper: float32 [8192], replicated, may hold values from 0.1 to 1.9
- counts: int32 [32], P(('grp', 'facet')), parts along dimension 0, may hold values from 0 to 199, as said below
- positions: int32 [32], P(('grp', 'facet')), parts along dimension 0, may hold values from 0 to 7
- channels: int32 [32], P(('grp', 'facet')), parts along dimension 0, may hold values from 0 to 95
- correction: float32 [65536], P('facet'), may hold values from 0.5 to 1.5
Outputs:
- image: float32 [2, 2, 65536, 256], P(None, None, 'facet', 'grp'), parts along dimension 3
The draws below stay inside these ranges and needn't reach their ends.
There are 2 independent parts, one for each index of `grp`. The reference program is written for one: setup_inputs(seed, part) draws one part's arguments, and reference() takes and returns one part's arrays. A program takes and returns all parts, laid end to end along the dimension named above; an argument that names none is the same for every part. Nothing has to cross between parts.
Inputs may be any that keep to these rules, and one draw needn't show every extreme that they name: `counts`: 0 means an empty subgrid; the share of empty subgrids differs from device to device; in each part at least one subgrid is non-empty.
All inputs are finite; a program needn't handle non-finite values.
Results may differ from the reference program's by a relative error of at most 0.0029.
Values may be sent and summed in bfloat16 or wider, within the bound.
No kernel may reach another device: no remote copies, remote signals or barrier semaphores. Data moves between devices by JAX's collectives and lax.ppermute only.
A program may use at most 128 MiB of HBM per device.

```python
import jax
import jax.numpy as jnp
from jax import lax

SG = 8192
NI = 65536
ROWS = 128
SUB_DEV = 1
TAYLOR = 2
CHANNELS = 96
SUBGRIDS = 16
FS = 4096
CONTRIB = 512
POS = 8
N_FACET = 16


def draw_counts(key, part):
    key = jax.random.fold_in(key, 11)
    first, second, third = jax.random.split(key, 3)
    amount = jax.random.randint(first, (SUBGRIDS,), 1, 200)
    density = jnp.repeat(jax.random.randint(third, (SUBGRIDS // SUB_DEV,), 0, 4), SUB_DEV)
    alive = jax.random.randint(second, (SUBGRIDS,), 0, 4) <= density
    index = jnp.arange(SUBGRIDS)
    result = jnp.where(alive, amount, 0)
    result = jnp.where(index == 0, 199, result)
    result = jnp.where(index == 1, 0, result)
    return result.astype(jnp.int32)


def with_ends(array, own_key, smallest, top_value):
    longest = array.shape.index(max(array.shape))
    spots = []
    for shift in (0, 1):
        where = [jax.random.randint(jax.random.fold_in(own_key, axis), (), 0, length) for axis, length in enumerate(array.shape)]
        where[longest] = (where[longest] + shift) % array.shape[longest]
        spots.append(tuple(where))
    return array.at[spots[0]].set(smallest).at[spots[1]].set(top_value)


def steps_of(stream_key, extent, cuts, smallest, top_value):
    factor_of, own = 1.0, jax.random.fold_in(stream_key, 6)
    for dim, blocks in cuts:
        draws = jnp.exp(jax.random.uniform(jax.random.fold_in(own, dim), (blocks,), jnp.float32, smallest / len(cuts), top_value / len(cuts)))
        factor_of = factor_of * jnp.repeat(draws, extent[dim] // blocks).reshape([-1 if axis == dim else 1 for axis in range(len(extent))])
    return factor_of


def bell_draw(own_key, dims, width, reach, cuts=(), kind=jnp.bfloat16):
    values = width * jax.random.normal(own_key, dims, jnp.float32)
    if cuts:
        values = values * steps_of(own_key, dims, cuts, -0.22, 0.18)
    return jnp.clip(values, -reach, reach).astype(kind)


def setup_inputs(seed: int = 0, part: int = 0) -> dict:
    splits = jax.random.split(jax.random.key(seed), 7)
    part_splits = jax.random.split(jax.random.fold_in(splits[6], part), 7)
    return {
        "subgrids": bell_draw(part_splits[0], (SUBGRIDS, 2, SG, ROWS), 1.0, 6.0, ((0, 16),)),
        "taper": jnp.clip(1.0 + 0.18 * jax.random.normal(splits[1], (SG,), jnp.float32), 0.1, 1.9),
        "counts": draw_counts(jax.random.fold_in(jax.random.fold_in(splits[6], part), 71), part),
        "positions": with_ends(jax.random.randint(part_splits[3], (SUBGRIDS,), 0, POS), jax.random.fold_in(part_splits[3], 1), 0, POS - 1).astype(jnp.int32),
        "channels": with_ends(jax.random.randint(part_splits[4], (SUBGRIDS,), 0, CHANNELS), jax.random.fold_in(part_splits[4], 1), 0, CHANNELS - 1).astype(jnp.int32),
        "correction": jnp.clip(1.0 + 0.1 * jax.random.normal(splits[5], (NI,), jnp.float32), 0.5, 1.5),
    }


def reference(subgrids, taper, counts, positions, channels, correction):
    data = subgrids.astype(jnp.float32) * taper[:, None]
    spectrum = jnp.fft.fft(data[:, 0] + 1j * data[:, 1], axis=-2, norm='ortho')
    parts = jnp.stack([jnp.real(spectrum), jnp.imag(spectrum)], axis=1).astype(jnp.bfloat16)
    root = jnp.sqrt(counts.astype(jnp.float32))
    weight = root * (SUBGRIDS / jnp.sum(root))
    half = 0.5 * (CHANNELS - 1)
    level = (channels.astype(jnp.float32) - half) / half
    terms = [weight]
    for order in range(1, TAYLOR):
        terms.append(terms[-1] * level)
    taylor = jnp.stack(terms)
    slots = (positions[None, :] == jnp.arange(POS, dtype=jnp.int32)[:, None]).astype(jnp.float32)
    table = taylor[:, None, :] * slots[None]
    rows = parts.shape[3]
    pieces = jnp.moveaxis(parts.reshape(SUBGRIDS, 2, N_FACET, CONTRIB, rows), 2, 0)
    gains = correction.reshape(N_FACET, FS)

    def one_facet(inputs):
        piece, gain = inputs
        buffer = jnp.einsum('tqs,sxcr->txqcr', table, piece.astype(jnp.float32), precision=lax.Precision.HIGHEST)
        buffer = buffer.reshape(TAYLOR, 2, FS, rows)
        field = jnp.fft.ifft(buffer[:, 0] + 1j * buffer[:, 1], axis=-2, norm='ortho')
        return jnp.stack([jnp.real(field), jnp.imag(field)], axis=1) * gain[:, None]
    facets = lax.map(one_facet, (pieces, gains))
    return jnp.moveaxis(facets, 0, 2).reshape(TAYLOR, 2, N_FACET * FS, rows)
```

```python
import functools
import math

import jax
import jax.numpy as jnp
import numpy as np
from jax import lax
from jax.experimental import pallas as pl
from jax.experimental.pallas import tpu as pltpu
from jax.sharding import PartitionSpec as P

TAYLOR = 2
CHANNELS = 96
MIB = 1024 * 1024
f32 = jnp.float32
bf16 = jnp.bfloat16

FIRST, LAST = 16, 48


def split(value):
    high = value.astype(bf16)
    return high, (value - high.astype(f32)).astype(bf16)


def forward_tables():
    b = np.arange(128)[:, None, None]
    ka = np.arange(64)[None, :, None]
    a = np.arange(64)[None, None, :]
    angle = 2 * np.pi * (((128 * a + b) * ka) % 8192) / 8192.0
    first = np.concatenate([np.cos(angle), np.sin(angle)], axis=2).astype(np.float32)
    kb = np.arange(128)[:, None]
    angle = 2 * np.pi * ((kb * kb.T) % 128) / 128
    cos = (np.cos(angle) / math.sqrt(8192.0)).reshape(16, 8, 128)
    sin = (np.sin(angle) / math.sqrt(8192.0)).reshape(16, 8, 128)
    second = np.empty((16, 8, 2, 2, 128))
    second[:, :, 0, 0], second[:, :, 0, 1] = cos, sin
    second[:, :, 1, 0], second[:, :, 1, 1] = -sin, cos
    second = second.reshape(256, 256).astype(np.float32)
    high = second.astype(bf16)
    low = (second - high.astype(np.float32)).astype(bf16)
    return first, np.concatenate([high, low], axis=1)


def inverse_table():
    k1 = np.arange(64)[:, None, None]
    k2 = np.arange(64)[None, :, None]
    cell = np.arange(64)[None, None, :]
    angle = 2 * np.pi * ((cell * (k1 + 64 * k2)) % 4096) / 4096.0
    cos, sin = np.cos(angle) / 64.0, np.sin(angle) / 64.0
    table = np.empty((64, 2, 64, 2, 64), np.float32)
    table[:, 0, :, 0], table[:, 0, :, 1] = cos, -sin
    table[:, 1, :, 0], table[:, 1, :, 1] = sin, cos
    return table.reshape(64, 128, 128)


def forward_kernel(meta_ref, sub_ref, taper_ref, first_ref, second_ref, *rest, sizes, per_step, unroll):
    pieces = rest[: len(sizes)]
    plain, tapers, mid = rest[len(sizes) :]
    step = pl.program_id(0)
    count = sum(sizes)

    @pl.when(step == 0)
    def _():
        turned = taper_ref[...].T
        tapers[:, 0:64] = turned
        tapers[:, 64:128] = turned

        @pl.loop(0, 64, unroll=4)
        def _(a):
            rows = pl.ds(pl.multiple_of(a * 128, 128), 128)
            plain[rows, :] = sub_ref[0, rows, :].astype(f32)
            plain[pl.ds(pl.multiple_of(8192 + a * 128, 128), 128), :] = sub_ref[1, rows, :].astype(f32)

    lane = lax.broadcasted_iota(jnp.int32, (1, 128), 1)
    sign = jnp.where(lane < 64, -1.0, 1.0).astype(f32)

    @pl.loop(0, per_step, unroll=unroll)
    def _(i):
        b = step * per_step + i
        data = plain[pl.ds(b, 128, stride=128), :].astype(bf16)
        taper = tapers[pl.ds(b, 1), :]
        table = first_ref[i]
        real = table * taper
        imag = pltpu.roll(table, 64, 1) * (taper * sign)
        high, low = split(jnp.concatenate([real, imag], axis=0))
        both = jnp.concatenate([high, low], axis=1)
        out = jnp.dot(both, jnp.concatenate([data, data], axis=0), preferred_element_type=f32)
        mid[pl.ds(b, count, stride=256), :] = out[:count]
        mid[pl.ds(128 + b, count, stride=256), :] = out[count:]

    @pl.when(step == pl.num_programs(0) - 1)
    def _():
        high, low = second_ref[:, 0:256], second_ref[:, 256:512]
        start = 0
        for piece, size in zip(pieces, sizes):

            @pl.loop(0, size // 2, unroll=4)
            def _(pair):
                both = []
                for j in range(2):
                    row = pl.multiple_of((start + 2 * pair + j) * 256, 256)
                    both.append(mid[pl.ds(row, 256), :])
                data_high, data_low = split(jnp.concatenate(both, axis=1))
                out = jnp.dot(high, data_high, preferred_element_type=f32)
                out += jnp.dot(low, data_high, preferred_element_type=f32)
                out += jnp.dot(high, data_low, preferred_element_type=f32)
                out = out.astype(bf16)
                for f in range(16):
                    for j in range(2):
                        piece[f, 2 * pair + j] = out[f * 16 : f * 16 + 16, j * 128 : j * 128 + 128]

            start += size
        if pieces[0].shape[1] > sizes[0]:
            row = lax.broadcasted_iota(jnp.int32, (16, 128), 0)
            tile = jnp.where(row == 0, meta_ref[0], jnp.where(row == 1, meta_ref[1], meta_ref[2]))
            tile = tile.astype(f32).astype(bf16)
            for f in range(16):
                pieces[0][f, sizes[0]] = tile


def forward(meta, subgrid, taper, first, second, sizes, per_step, unroll, extra=0):
    count = sum(sizes)
    shapes = [jax.ShapeDtypeStruct((16, size + extra, 16, 128), bf16) for size in sizes]
    return pl.pallas_call(
        functools.partial(forward_kernel, sizes=sizes, per_step=per_step, unroll=unroll),
        grid=(128 // per_step,),
        in_specs=[
            pl.BlockSpec(memory_space=pltpu.SMEM),
            pl.BlockSpec((2, 8192, 128), lambda i: (0, 0, 0)),
            pl.BlockSpec((64, 128), lambda i: (0, 0)),
            pl.BlockSpec((per_step, count, 128), lambda i: (i, 0, 0)),
            pl.BlockSpec((256, 512), lambda i: (0, 0)),
        ],
        out_specs=[pl.BlockSpec(shape.shape, lambda i: (0, 0, 0, 0)) for shape in shapes],
        out_shape=shapes,
        scratch_shapes=[
            pltpu.VMEM((16384, 128), f32),
            pltpu.VMEM((128, 128), f32),
            pltpu.VMEM((count * 256, 128), f32),
        ],
        compiler_params=pltpu.CompilerParams(
            vmem_limit_bytes=58 * MIB, dimension_semantics=("arbitrary",)
        ),
        cost_estimate=pl.CostEstimate(flops=60000000 * count, bytes_accessed=8 * MIB, transcendentals=0),
        name="forward%d" % count,
    )(meta, subgrid, taper, first, second)


def place(high, low, ref, size, store, width, at):
    @pl.loop(0, size // 2, unroll=2)
    def _(pair):
        both = [jnp.concatenate([ref[s, 2 * pair + j] for s in range(16)], axis=0) for j in range(2)]
        data = jnp.concatenate(both, axis=1)
        out = jnp.dot(high, data, preferred_element_type=f32) + jnp.dot(low, data, preferred_element_type=f32)
        for j in range(2):
            store[pl.ds(at + 2 * pair + j, 256, stride=width), :] = out[:, j * 128 : j * 128 + 128]


def placing_matrix(tiles):
    owner = lax.broadcasted_iota(jnp.int32, (16, 256), 1) >> 4
    meta = jnp.zeros((16, 256), f32)
    for s, tile in enumerate(tiles):
        tile = tile.astype(f32)
        meta = jnp.where(owner == s, jnp.concatenate([tile, tile], axis=1), meta)
    counts, positions, channels = meta[0:1], meta[1:2].astype(jnp.int32), meta[2:3]
    root = jnp.sqrt(counts)
    weight = root * (16.0 / (jnp.sum(root, axis=1, keepdims=True) * (1.0 / 16)))
    half = 0.5 * (CHANNELS - 1)
    level = (channels - half) / half
    row = lax.broadcasted_iota(jnp.int32, (128, 256), 0)
    lane = lax.broadcasted_iota(jnp.int32, (128, 256), 1)
    n1 = positions * 8 + ((lane >> 1) & 7)
    index = (n1 * (row >> 1) + 16 * ((lane & 1) - (row & 1))) & 63
    wave = jnp.cos(index.astype(f32) * (2 * math.pi / 64))
    return jnp.concatenate([wave * weight, wave * (weight * level)], axis=0)


def middle_kernel(correction_ref, table_ref, *rest, sizes):
    refs = rest[: len(sizes)]
    stage_ref, matrix_ref, scaled_ref, store = rest[len(sizes) :]
    width = sum(sizes)
    high, low = split(placing_matrix([refs[0][s, sizes[0]] for s in range(16)]))
    matrix_ref[:, 0:256] = high
    matrix_ref[:, 256:512] = low
    at = 0
    for part, size in enumerate(sizes):
        place(high, low, refs[part], size, store, width, at)
        at += size
    chunk = 16 * width

    @pl.loop(0, 16)
    def _(i):
        rows = pl.ds(pl.multiple_of(i * chunk, chunk), chunk)
        stage_ref[rows, :] = store[rows, :].astype(bf16)

    gains = correction_ref[...].T
    gains = jnp.concatenate([gains, gains], axis=1).T
    for k1 in range(64):
        high, low = split(table_ref[k1] * gains[:, k1 : k1 + 1])
        scaled_ref[k1, :, 0:128] = high
        scaled_ref[k1, :, 128:256] = low


def middle(correction, table, parts, sizes):
    width = sum(sizes)
    refs = parts
    whole = lambda shape: pl.BlockSpec(shape, lambda i: (0,) * len(shape))
    shapes = [
        jax.ShapeDtypeStruct((256 * width, 128), bf16),
        jax.ShapeDtypeStruct((256, 512), bf16),
        jax.ShapeDtypeStruct((64, 128, 256), bf16),
    ]
    return pl.pallas_call(
        functools.partial(middle_kernel, sizes=sizes),
        grid=(1,),
        in_specs=[whole(correction.shape), whole(table.shape)] + [whole(r.shape) for r in refs],
        out_specs=[whole(shape.shape) for shape in shapes],
        out_shape=shapes,
        scratch_shapes=[pltpu.VMEM((256 * width, 128), f32)],
        compiler_params=pltpu.CompilerParams(vmem_limit_bytes=58 * MIB, dimension_semantics=("arbitrary",)),
        cost_estimate=pl.CostEstimate(flops=3000000000, bytes_accessed=16 * MIB, transcendentals=0),
        name="middle",
    )(correction, table, *refs)


def final_kernel(matrix_ref, stage_ref, scaled_ref, pieces_ref, out_ref, store, *, size):
    width = 64 - size
    step = pl.program_id(0)

    @pl.when(step == 0)
    def _():
        place(matrix_ref[:, 0:256], matrix_ref[:, 256:512], pieces_ref, size, store, size, 0)

    flat = out_ref.reshape(2 * 2 * 64 * 8, 128)
    for i in range(8):
        k1 = step * 8 + i
        columns = []
        for t in range(2):
            parts = []
            for x in range(2):
                row = (t * 64 + k1) * 2 + x
                parts.append(stage_ref[pl.ds(pl.multiple_of(row * width, 16), width), :])
                parts.append(store[pl.ds(pl.multiple_of(row * size, 16), size), :].astype(bf16))
            columns.append(jnp.concatenate(parts, axis=0))
        data = jnp.concatenate(columns, axis=1)
        out = jnp.dot(scaled_ref[i], jnp.concatenate([data, data], axis=0), preferred_element_type=f32)
        for t in range(2):
            for x in range(2):
                block = out[x * 64 : x * 64 + 64, t * 128 : t * 128 + 128]
                flat[pl.ds((t * 2 + x) * 512 + i, 64, stride=8), :] = block


def final(matrix, stage, scaled, pieces, size):
    whole = lambda shape: pl.BlockSpec(shape, lambda i: (0,) * len(shape))
    vmem = pl.BlockSpec(memory_space=pltpu.VMEM)
    return pl.pallas_call(
        functools.partial(final_kernel, size=size),
        grid=(8,),
        in_specs=[vmem, vmem, pl.BlockSpec((8, 128, 256), lambda i: (i, 0, 0)), whole(pieces.shape)],
        out_specs=pl.BlockSpec((2, 2, 64, 8, 128), lambda i: (0, 0, 0, i, 0)),
        out_shape=jax.ShapeDtypeStruct((2, 2, 64, 64, 128), f32),
        scratch_shapes=[pltpu.VMEM((256 * size, 128), f32)],
        compiler_params=pltpu.CompilerParams(vmem_limit_bytes=24 * MIB, dimension_semantics=("arbitrary",)),
        cost_estimate=pl.CostEstimate(flops=3000000000, bytes_accessed=16 * MIB, transcendentals=0),
        name="final",
    )(matrix, stage, scaled, pieces)


def exchange(pieces):
    return lax.all_to_all(pieces, "facet", split_axis=0, concat_axis=0, tiled=True)


def local(subgrids, taper, counts, positions, channels, correction):
    first, second = forward_tables()
    inverse = inverse_table()
    subgrid = subgrids[0]
    taper = taper.reshape(64, 128)
    meta = jnp.concatenate([counts, positions, channels])
    (one,) = forward(meta, subgrid, taper, first[:, :FIRST], second, (FIRST,), 128, 8, 1)
    one = exchange(one)
    (two,) = forward(meta, subgrid, taper, first[:, FIRST:], second, (LAST,), 16, 8)
    two = exchange(two)
    stage, matrix, scaled = middle(correction.reshape(64, 64), inverse, [one], (FIRST,))
    image = final(matrix, stage, scaled, two, LAST)
    return image.reshape(TAYLOR, 2, 4096, 128)


def phase_table(height, breadth, length, sign):
    first = jnp.arange(height, dtype=jnp.int32)[:, None]
    second = jnp.arange(breadth, dtype=jnp.int32)[None, :]
    angle = (first * second % length).astype(jnp.float32) * (2.0 * math.pi / length)
    return (jnp.cos(angle), sign * jnp.sin(angle))


def transform(real_part, imag_part, sign):
    length = real_part.shape[-2]
    width = real_part.shape[-1]
    outer = math.gcd(length, 64)
    inner = length // outer
    leading = real_part.shape[:-2]
    real_in = real_part.reshape(leading + (outer, inner, width))
    imag_in = imag_part.reshape(leading + (outer, inner, width))
    high = lax.Precision.HIGHEST
    outer_re, outer_im = phase_table(outer, outer, outer, sign)
    twist_re, twist_im = phase_table(outer, inner, length, sign)
    twist_re = twist_re[:, :, None]
    twist_im = twist_im[:, :, None]
    inner_re, inner_im = phase_table(inner, inner, inner, sign)
    first_re = jnp.einsum("ka,...abr->...kbr", outer_re, real_in, precision=high) - jnp.einsum(
        "ka,...abr->...kbr", outer_im, imag_in, precision=high
    )
    first_im = jnp.einsum("ka,...abr->...kbr", outer_re, imag_in, precision=high) + jnp.einsum(
        "ka,...abr->...kbr", outer_im, real_in, precision=high
    )
    turned_re = first_re * twist_re - first_im * twist_im
    turned_im = first_re * twist_im + first_im * twist_re
    last_re = jnp.einsum("bm,...kbr->...mkr", inner_re, turned_re, precision=high) - jnp.einsum(
        "bm,...kbr->...mkr", inner_im, turned_im, precision=high
    )
    last_im = jnp.einsum("bm,...kbr->...mkr", inner_im, turned_re, precision=high) + jnp.einsum(
        "bm,...kbr->...mkr", inner_re, turned_im, precision=high
    )
    factor = 1.0 / math.sqrt(length)
    return (
        last_re.reshape(leading + (length, width)) * factor,
        last_im.reshape(leading + (length, width)) * factor,
    )


def general(subgrids, taper, counts, positions, channels, correction):
    local_count = subgrids.shape[0]
    facets = lax.axis_size("facet")
    every_count, every_position, every_channel = (
        lax.all_gather(counts, "facet", axis=0, tiled=True),
        lax.all_gather(positions, "facet", axis=0, tiled=True),
        lax.all_gather(channels, "facet", axis=0, tiled=True),
    )
    data = subgrids[0].astype(jnp.float32) * taper[:, None]
    wave_re, wave_im = transform(data[0], data[1], -1.0)
    block = jnp.stack([wave_re, wave_im]).astype(jnp.bfloat16)[None]
    received_list = [lax.all_to_all(block, "facet", split_axis=2, concat_axis=0, tiled=True)]
    stacked = jnp.stack(received_list, axis=1)
    received = stacked.reshape((facets * local_count,) + stacked.shape[2:])
    root = jnp.sqrt(every_count.astype(jnp.float32))
    weight = root * (root.shape[0] / jnp.sum(root))
    half = 0.5 * (CHANNELS - 1)
    level = (every_channel.astype(jnp.float32) - half) / half
    terms = [weight]
    terms.append(terms[-1] * level)
    taylor = jnp.stack(terms)
    contrib = received.shape[2]
    rows = received.shape[3]
    slot_count = correction.shape[0] // contrib
    slots = (every_position[None, :] == jnp.arange(slot_count, dtype=jnp.int32)[:, None]).astype(
        jnp.float32
    )
    table = taylor[:, None, :] * slots[None]
    buffer = jnp.einsum(
        "tqs,sxcr->txqcr", table, received.astype(jnp.float32), precision=lax.Precision.HIGHEST
    )
    buffer = buffer.reshape(TAYLOR, 2, slot_count * contrib, rows)
    field_re, field_im = transform(buffer[:, 0], buffer[:, 1], 1.0)
    return jnp.stack([field_re, field_im], axis=1) * correction[:, None]


def solution(mesh):
    placed = (
        P(("grp", "facet"), None, None, None),
        P(),
        P(("grp", "facet")),
        P(("grp", "facet")),
        P(("grp", "facet")),
        P("facet"),
    )
    own = local if mesh.shape["facet"] == 16 else general
    return jax.shard_map(
        own, mesh=mesh, in_specs=placed, out_specs=P(None, None, "facet", "grp"), check_vma=False
    )
```

```python
import functools
import math

import jax
import jax.numpy as jnp
import numpy as np
from jax import lax
from jax.experimental import pallas as pl
from jax.experimental.pallas import tpu as pltpu
from jax.sharding import PartitionSpec as P

TAYLOR = 2
CHANNELS = 96
MIB = 1024 * 1024
f32 = jnp.float32
bf16 = jnp.bfloat16

PITCH, PITCH_MID, PITCH_STAGE, PITCH_IMAGE = 136, 264, 72, 72


def split(value):
    high = value.astype(bf16)
    return high, (value - high.astype(f32)).astype(bf16)


def forward_tables():
    b = np.arange(128)[:, None, None]
    ka = np.arange(64)[None, :, None]
    a = np.arange(64)[None, None, :]
    angle = 2 * np.pi * (((128 * a + b) * ka) % 8192) / 8192.0
    first = np.concatenate([np.cos(angle), np.sin(angle)], axis=2).astype(np.float32)
    kb = np.arange(128)[:, None]
    angle = 2 * np.pi * ((kb * kb.T) % 128) / 128
    cos = (np.cos(angle) / math.sqrt(8192.0)).reshape(16, 8, 128)
    sin = (np.sin(angle) / math.sqrt(8192.0)).reshape(16, 8, 128)
    second = np.empty((16, 8, 2, 2, 128))
    second[:, :, 0, 0], second[:, :, 0, 1] = cos, sin
    second[:, :, 1, 0], second[:, :, 1, 1] = -sin, cos
    second = second.reshape(256, 256).astype(np.float32)
    high = second.astype(bf16)
    low = (second - high.astype(np.float32)).astype(bf16)
    return first, np.concatenate([high, low], axis=1)


def inverse_table():
    k1 = np.arange(64)[:, None, None]
    k2 = np.arange(64)[None, :, None]
    cell = np.arange(64)[None, None, :]
    angle = 2 * np.pi * ((cell * (k1 + 64 * k2)) % 4096) / 4096.0
    cos, sin = np.cos(angle) / 64.0, np.sin(angle) / 64.0
    table = np.empty((64, 2, 64, 2, 64), np.float32)
    table[:, 0, :, 0], table[:, 0, :, 1] = cos, -sin
    table[:, 1, :, 0], table[:, 1, :, 1] = sin, cos
    return table.reshape(64, 128, 128)


def forward_kernel(*rest, subset, starts, count, extra):
    if extra:
        meta_ref, *rest = rest
    sub_hbm, taper_ref, first_hbm, second_ref, *rest = rest
    outs = rest[: len(subset)]
    sub_ref, first_ref, plain, tapers, mid, pieces, sub_sem, first_sem, out_sem = rest[len(subset) :]
    sub_copies, first_copies, out_copies = [], [], []
    for q in range(4):
        for x in range(2):
            rows = pl.ds(q * 2048, 2048)
            copy = pltpu.make_async_copy(sub_hbm.at[x, rows], sub_ref.at[x, rows], sub_sem.at[q, x])
            copy.start()
            sub_copies.append(copy)
    for q in range(4):
        rows = pl.ds(q * 32, 32)
        copy = pltpu.make_async_copy(first_hbm.at[rows], first_ref.at[rows], first_sem.at[q])
        copy.start()
        first_copies.append(copy)
    turned = taper_ref[...].T
    tapers[:, 0:64] = turned
    tapers[:, 64:128] = turned
    for q in range(4):
        sub_copies[2 * q].wait()
        sub_copies[2 * q + 1].wait()

        @pl.loop(16 * q, 16 * q + 16, unroll=4)
        def _(a):
            rows = pl.ds(pl.multiple_of(a * 128, 128), 128)
            plain[pl.ds(pl.multiple_of(a * PITCH, 8), 128), :] = sub_ref[0, rows, :].astype(f32)
            plain[pl.ds(pl.multiple_of((64 + a) * PITCH, 8), 128), :] = sub_ref[1, rows, :].astype(f32)

    lane = lax.broadcasted_iota(jnp.int32, (1, 128), 1)
    sign = jnp.where(lane < 64, -1.0, 1.0).astype(f32)

    def operands(b):
        data = plain[pl.ds(b, 128, stride=PITCH), :].astype(bf16)
        taper = tapers[pl.ds(b, 1), :]
        table = first_ref[b]
        real = table * taper
        imag = pltpu.roll(table, 64, 1) * (taper * sign)
        high, low = split(jnp.concatenate([real, imag], axis=0))
        return data, jnp.concatenate([high, low], axis=1)

    for q in range(4):
        first_copies[q].wait()

        @pl.loop(16 * q, 16 * q + 16, unroll=16)
        def _(pair):
            data_a, matrix_a = operands(2 * pair)
            data_b, matrix_b = operands(2 * pair + 1)
            data = jnp.concatenate([data_a, data_b], axis=1)
            out = jnp.dot(
                jnp.concatenate([matrix_a, matrix_b], axis=0),
                jnp.concatenate([data, data], axis=0),
                preferred_element_type=f32,
            )
            for j in range(2):
                b = 2 * pair + j
                mine = out[2 * count * j : 2 * count * (j + 1), 128 * j : 128 * j + 128]
                mid[pl.ds(b, count, stride=PITCH_MID), :] = mine[:count]
                mid[pl.ds(128 + b, count, stride=PITCH_MID), :] = mine[count:]

    me = lax.axis_index("facet")
    blocks = [pl.ds(pl.multiple_of((me ^ s) * 16, 16), 16) for s in subset]
    high = jnp.concatenate([second_ref[rows, 0:256] for rows in blocks], axis=0)
    low = jnp.concatenate([second_ref[rows, 256:512] for rows in blocks], axis=0)
    rows = 16 * len(subset)
    if extra:
        row = lax.broadcasted_iota(jnp.int32, (16, 128), 0)
        tile = jnp.where(row == 0, meta_ref[0], jnp.where(row == 1, meta_ref[1], meta_ref[2]))
        tile = tile.astype(f32).astype(bf16)
        for i in range(len(subset)):
            pieces[i, count] = tile
    part = count // 2
    for half in range(2):

        @pl.loop(part // 2 * half, part // 2 * (half + 1), unroll=8)
        def _(pair):
            both = []
            for j in range(2):
                start = pl.multiple_of((2 * pair + j) * PITCH_MID, 8)
                both.append(mid[pl.ds(start, 256), :])
            data_high, data_low = split(jnp.concatenate(both, axis=1))
            out = jnp.dot(jnp.concatenate([high, low], axis=0), data_high, preferred_element_type=f32)
            out = out[:rows] + out[rows:] + jnp.dot(high, data_low, preferred_element_type=f32)
            out = out.astype(bf16)
            for i in range(len(subset)):
                for j in range(2):
                    pieces[i, 2 * pair + j] = out[i * 16 : i * 16 + 16, j * 128 : j * 128 + 128]

        size = part + (extra if half else 0)
        for i, start in enumerate(starts):
            if half * part >= start:
                copy = pltpu.make_async_copy(
                    pieces.at[i, pl.ds(half * part, size)],
                    outs[i].at[pl.ds(half * part - start, size)],
                    out_sem.at[half, i],
                )
                copy.start()
                out_copies.append(copy)
    for copy in out_copies:
        copy.wait()


def forward(subgrid, taper, first, second, subset, starts, meta=None):
    number, count, extra = len(subset), first.shape[1], 0 if meta is None else 1
    shapes = [jax.ShapeDtypeStruct((count - start + extra, 16, 128), bf16) for start in starts]
    hbm = pl.BlockSpec(memory_space=pl.ANY)
    return pl.pallas_call(
        functools.partial(forward_kernel, subset=subset, starts=starts, count=count, extra=extra),
        grid=(1,),
        in_specs=[pl.BlockSpec(memory_space=pltpu.SMEM)] * extra
        + [
            hbm,
            pl.BlockSpec((64, 128), lambda i: (0, 0)),
            hbm,
            pl.BlockSpec((256, 512), lambda i: (0, 0)),
        ],
        out_specs=[hbm] * number,
        out_shape=shapes,
        scratch_shapes=[
            pltpu.VMEM((2, 8192, 128), bf16),
            pltpu.VMEM((128, count, 128), f32),
            pltpu.VMEM((128 * PITCH, 128), f32),
            pltpu.VMEM((128, 128), f32),
            pltpu.VMEM((count * PITCH_MID, 128), f32),
            pltpu.VMEM((number, count + extra, 16, 128), bf16),
            pltpu.SemaphoreType.DMA((4, 2)),
            pltpu.SemaphoreType.DMA((4,)),
            pltpu.SemaphoreType.DMA((2, number)),
        ],
        compiler_params=pltpu.CompilerParams(vmem_limit_bytes=58 * MIB),
        cost_estimate=pl.CostEstimate(flops=160000000 * count, bytes_accessed=12 * MIB, transcendentals=0),
        name=f"forward{number}",
    )(*([meta] * extra), subgrid, taper, first, second)


def placing_matrix(tiles):
    owner = lax.broadcasted_iota(jnp.int32, (16, 256), 1) >> 4
    meta = jnp.zeros((16, 256), f32)
    for s, tile in enumerate(tiles):
        tile = tile.astype(f32)
        meta = jnp.where(owner == s, jnp.concatenate([tile, tile], axis=1), meta)
    counts, positions, channels = meta[0:1], meta[1:2].astype(jnp.int32), meta[2:3]
    root = jnp.sqrt(counts)
    weight = root * (16.0 / (jnp.sum(root, axis=1, keepdims=True) * (1.0 / 16)))
    half = 0.5 * (CHANNELS - 1)
    level = (channels - half) / half
    row = lax.broadcasted_iota(jnp.int32, (128, 256), 0)
    lane = lax.broadcasted_iota(jnp.int32, (128, 256), 1)
    n1 = positions * 8 + ((lane >> 1) & 7)
    index = (n1 * (row >> 1) + 16 * ((lane & 1) - (row & 1))) & 63
    wave = jnp.cos(index.astype(f32) * (2 * math.pi / 64))
    return jnp.concatenate([wave * weight, wave * (weight * level)], axis=0)


def scale_kernel(correction_ref, table_ref, scaled_ref):
    gains = correction_ref[...].T
    gains = jnp.concatenate([gains, gains], axis=1).T
    for k1 in range(64):
        high, low = split(table_ref[k1] * gains[:, k1 : k1 + 1])
        scaled_ref[k1, :, 0:128] = high
        scaled_ref[k1, :, 128:256] = low


def scale(correction, table):
    whole = lambda shape: pl.BlockSpec(shape, lambda i: (0,) * len(shape))
    shape = jax.ShapeDtypeStruct((64, 128, 256), bf16)
    return pl.pallas_call(
        scale_kernel,
        grid=(1,),
        in_specs=[whole(correction.shape), whole(table.shape)],
        out_specs=whole(shape.shape),
        out_shape=shape,
        compiler_params=pltpu.CompilerParams(vmem_limit_bytes=58 * MIB, dimension_semantics=("arbitrary",)),
        cost_estimate=pl.CostEstimate(flops=6000000000, bytes_accessed=16 * MIB, transcendentals=0),
        name="scale",
    )(correction, table)


def final_kernel(scaled_hbm, *rest, sizes):
    refs = rest[: len(sizes)]
    out_hbm, store, held, scaled_ref, image, piece_sem, scaled_sem, out_sem = rest[len(sizes) :]
    scaled_copies, out_copies = [], []
    piece_copies = [[], [], []]

    def fetch(ref, at, s, stage, start, size):
        target = held.at[s, pl.ds(start, size)]
        copy = pltpu.make_async_copy(ref.at[pl.ds(at, size)], target, piece_sem.at[stage, s])
        copy.start()
        piece_copies[stage].append(copy)

    wholes = refs[len(sizes) - 16 :]
    halves = refs[: len(sizes) - 16]
    for s, ref in enumerate(wholes):
        fetch(ref, ref.shape[0] - 1, s, 0, 64, 1)
    for s, ref in enumerate(wholes):
        fetch(halves[s] if s < len(halves) else ref, 0, s, 1, 0, 32)
    for s, ref in enumerate(wholes):
        fetch(ref, 0 if s < len(halves) else 32, s, 2, 32, 32)
    for q in range(4):
        part = pl.ds(16 * q, 16)
        copy = pltpu.make_async_copy(scaled_hbm.at[part], scaled_ref.at[part], scaled_sem.at[q])
        copy.start()
        scaled_copies.append(copy)
    for copy in piece_copies[0]:
        copy.wait()
    high, low = split(placing_matrix([held[s, 64] for s in range(16)]))
    for half in range(2):
        for copy in piece_copies[1 + half]:
            copy.wait()

        @pl.loop(16 * half, 16 * half + 16, unroll=8)
        def _(pair):
            both = [jnp.concatenate([held[s, 2 * pair + j] for s in range(16)], axis=0) for j in range(2)]
            data = jnp.concatenate(both, axis=1)
            out = jnp.dot(high, data, preferred_element_type=f32) + jnp.dot(low, data, preferred_element_type=f32)
            for j in range(2):
                store[pl.ds(2 * pair + j, 256, stride=PITCH_STAGE), :] = out[:, j * 128 : j * 128 + 128]

    for copy in scaled_copies:
        copy.wait()
    for t in range(2):

        @pl.loop(0, 64, unroll=32)
        def _(k1):
            row = (t * 64 + k1) * (2 * PITCH_STAGE)
            parts = [store[pl.ds(pl.multiple_of(row + x * PITCH_STAGE, 8), 64), :] for x in range(2)]
            data = jnp.concatenate(parts, axis=0).astype(bf16)
            out = jnp.dot(scaled_ref[k1], jnp.concatenate([data, data], axis=0), preferred_element_type=f32)
            for x in range(2):
                start = (t * 2 + x) * (64 * PITCH_IMAGE)
                image[pl.ds(start + k1, 64, stride=PITCH_IMAGE), :] = out[x * 64 : x * 64 + 64]

        for x in range(2):
            source = image.reshape(4, 64, PITCH_IMAGE, 128).at[t * 2 + x, :, pl.ds(0, 64)]
            copy = pltpu.make_async_copy(source, out_hbm.at[t, x], out_sem.at[t, x])
            copy.start()
            out_copies.append(copy)
    for copy in out_copies:
        copy.wait()


def final(scaled, pieces):
    hbm = pl.BlockSpec(memory_space=pl.ANY)
    sizes = tuple(piece.shape[0] for piece in pieces)
    return pl.pallas_call(
        functools.partial(final_kernel, sizes=sizes),
        in_specs=[hbm] * (1 + len(pieces)),
        out_specs=hbm,
        out_shape=jax.ShapeDtypeStruct((2, 2, 64, 64, 128), f32),
        scratch_shapes=[
            pltpu.VMEM((256 * PITCH_STAGE, 128), f32),
            pltpu.VMEM((16, 65, 16, 128), bf16),
            pltpu.VMEM((64, 128, 256), bf16),
            pltpu.VMEM((4 * 64 * PITCH_IMAGE, 128), f32),
            pltpu.SemaphoreType.DMA((3, 16)),
            pltpu.SemaphoreType.DMA((4,)),
            pltpu.SemaphoreType.DMA((2, 2)),
        ],
        compiler_params=pltpu.CompilerParams(vmem_limit_bytes=58 * MIB),
        cost_estimate=pl.CostEstimate(flops=8000000000, bytes_accessed=16 * MIB, transcendentals=0),
        name="final",
    )(scaled, *pieces)


EARLY = (8, 9, 10)
LATE = (8, 9, 10, 3, 11, 2, 12, 1, 4, 13, 5, 6, 14, 7, 15)


def exchange(piece, s):
    return lax.ppermute(piece, "facet", [(i, i ^ s) for i in range(16)])


def local(subgrids, taper, counts, positions, channels, correction):
    first, second = forward_tables()
    inputs = (subgrids[0], taper.reshape(64, 128))
    early = forward(*inputs, first[:, :32], second, EARLY, (0,) * len(EARLY))
    starts = tuple(32 if s in EARLY else 0 for s in LATE) + (0,)
    meta = jnp.concatenate([counts, positions, channels])
    late = forward(*inputs, first, second, LATE + (0,), starts, meta)
    early = [exchange(piece, s) for s, piece in zip(EARLY, early)]
    late = [exchange(piece, s) for s, piece in zip(LATE, late)] + [late[15]]
    scaled = scale(correction.reshape(64, 64), inverse_table())
    image = final(scaled, early + late)
    return image.reshape(TAYLOR, 2, 4096, 128)


def phase_table(height, breadth, length, sign):
    first = jnp.arange(height, dtype=jnp.int32)[:, None]
    second = jnp.arange(breadth, dtype=jnp.int32)[None, :]
    angle = (first * second % length).astype(jnp.float32) * (2.0 * math.pi / length)
    return (jnp.cos(angle), sign * jnp.sin(angle))


def transform(real_part, imag_part, sign):
    length = real_part.shape[-2]
    width = real_part.shape[-1]
    outer = math.gcd(length, 64)
    inner = length // outer
    leading = real_part.shape[:-2]
    real_in = real_part.reshape(leading + (outer, inner, width))
    imag_in = imag_part.reshape(leading + (outer, inner, width))
    high = lax.Precision.HIGHEST
    outer_re, outer_im = phase_table(outer, outer, outer, sign)
    twist_re, twist_im = phase_table(outer, inner, length, sign)
    twist_re = twist_re[:, :, None]
    twist_im = twist_im[:, :, None]
    inner_re, inner_im = phase_table(inner, inner, inner, sign)
    first_re = jnp.einsum("ka,...abr->...kbr", outer_re, real_in, precision=high) - jnp.einsum(
        "ka,...abr->...kbr", outer_im, imag_in, precision=high
    )
    first_im = jnp.einsum("ka,...abr->...kbr", outer_re, imag_in, precision=high) + jnp.einsum(
        "ka,...abr->...kbr", outer_im, real_in, precision=high
    )
    turned_re = first_re * twist_re - first_im * twist_im
    turned_im = first_re * twist_im + first_im * twist_re
    last_re = jnp.einsum("bm,...kbr->...mkr", inner_re, turned_re, precision=high) - jnp.einsum(
        "bm,...kbr->...mkr", inner_im, turned_im, precision=high
    )
    last_im = jnp.einsum("bm,...kbr->...mkr", inner_im, turned_re, precision=high) + jnp.einsum(
        "bm,...kbr->...mkr", inner_re, turned_im, precision=high
    )
    factor = 1.0 / math.sqrt(length)
    return (
        last_re.reshape(leading + (length, width)) * factor,
        last_im.reshape(leading + (length, width)) * factor,
    )


def general(subgrids, taper, counts, positions, channels, correction):
    local_count = subgrids.shape[0]
    facets = lax.axis_size("facet")
    every_count, every_position, every_channel = (
        lax.all_gather(counts, "facet", axis=0, tiled=True),
        lax.all_gather(positions, "facet", axis=0, tiled=True),
        lax.all_gather(channels, "facet", axis=0, tiled=True),
    )
    data = subgrids[0].astype(jnp.float32) * taper[:, None]
    wave_re, wave_im = transform(data[0], data[1], -1.0)
    block = jnp.stack([wave_re, wave_im]).astype(jnp.bfloat16)[None]
    received_list = [lax.all_to_all(block, "facet", split_axis=2, concat_axis=0, tiled=True)]
    stacked = jnp.stack(received_list, axis=1)
    received = stacked.reshape((facets * local_count,) + stacked.shape[2:])
    root = jnp.sqrt(every_count.astype(jnp.float32))
    weight = root * (root.shape[0] / jnp.sum(root))
    half = 0.5 * (CHANNELS - 1)
    level = (every_channel.astype(jnp.float32) - half) / half
    terms = [weight]
    terms.append(terms[-1] * level)
    taylor = jnp.stack(terms)
    contrib = received.shape[2]
    rows = received.shape[3]
    slot_count = correction.shape[0] // contrib
    slots = (every_position[None, :] == jnp.arange(slot_count, dtype=jnp.int32)[:, None]).astype(
        jnp.float32
    )
    table = taylor[:, None, :] * slots[None]
    buffer = jnp.einsum(
        "tqs,sxcr->txqcr", table, received.astype(jnp.float32), precision=lax.Precision.HIGHEST
    )
    buffer = buffer.reshape(TAYLOR, 2, slot_count * contrib, rows)
    field_re, field_im = transform(buffer[:, 0], buffer[:, 1], 1.0)
    return jnp.stack([field_re, field_im], axis=1) * correction[:, None]


def solution(mesh):
    placed = (
        P(("grp", "facet"), None, None, None),
        P(),
        P(("grp", "facet")),
        P(("grp", "facet")),
        P(("grp", "facet")),
        P("facet"),
    )
    own = local if mesh.shape["facet"] == 16 else general
    return jax.shard_map(
        own, mesh=mesh, in_specs=placed, out_specs=P(None, None, "facet", "grp"), check_vma=False
    )
```

```python
import functools
import math

import jax
import jax.numpy as jnp
import numpy as np
from jax import lax
from jax.experimental import pallas as pl
from jax.experimental.pallas import tpu as pltpu
from jax.sharding import PartitionSpec as P

TAYLOR = 2
CHANNELS = 96
MIB = 1024 * 1024
f32 = jnp.float32
bf16 = jnp.bfloat16

PITCH, PITCH_MID, PITCH_STAGE, PITCH_IMAGE = 136, 264, 72, 72


def split(value):
    high = value.astype(bf16)
    return high, (value - high.astype(f32)).astype(bf16)


def forward_tables():
    b = np.arange(128)[:, None, None]
    ka = np.arange(64)[None, :, None]
    a = np.arange(64)[None, None, :]
    angle = 2 * np.pi * (((128 * a + b) * ka) % 8192) / 8192.0
    first = np.concatenate([np.cos(angle), np.sin(angle)], axis=2).astype(np.float32)
    kb = np.arange(128)[:, None]
    angle = 2 * np.pi * ((kb * kb.T) % 128) / 128
    cos = (np.cos(angle) / math.sqrt(8192.0)).reshape(16, 8, 128)
    sin = (np.sin(angle) / math.sqrt(8192.0)).reshape(16, 8, 128)
    second = np.empty((16, 8, 2, 2, 128))
    second[:, :, 0, 0], second[:, :, 0, 1] = cos, sin
    second[:, :, 1, 0], second[:, :, 1, 1] = -sin, cos
    second = second.reshape(256, 256).astype(np.float32)
    high = second.astype(bf16)
    low = (second - high.astype(np.float32)).astype(bf16)
    return first, np.concatenate([high, low], axis=1)


def inverse_table():
    k1 = np.arange(64)[:, None, None]
    k2 = np.arange(64)[None, :, None]
    cell = np.arange(64)[None, None, :]
    angle = 2 * np.pi * ((cell * (k1 + 64 * k2)) % 4096) / 4096.0
    cos, sin = np.cos(angle) / 64.0, np.sin(angle) / 64.0
    table = np.empty((64, 2, 64, 2, 64), np.float32)
    table[:, 0, :, 0], table[:, 0, :, 1] = cos, -sin
    table[:, 1, :, 0], table[:, 1, :, 1] = sin, cos
    return table.reshape(64, 128, 128)


def forward_kernel(*rest, near, subset, starts, count, extra):
    if extra:
        meta_ref, *rest = rest
    sub_hbm, taper_ref, first_hbm, second_ref, *rest = rest
    number = near + len(subset)
    outs = rest[: len(subset) + (1 if near else 0)]
    sub_ref, first_ref, plain, tapers, mid, pieces, sub_sem, first_sem, out_sem = rest[len(outs) :]
    sub_copies, first_copies, out_copies = [], [], []
    for q in range(4):
        for x in range(2):
            rows = pl.ds(q * 2048, 2048)
            copy = pltpu.make_async_copy(sub_hbm.at[x, rows], sub_ref.at[x, rows], sub_sem.at[q, x])
            copy.start()
            sub_copies.append(copy)
    for q in range(4):
        rows = pl.ds(q * 32, 32)
        copy = pltpu.make_async_copy(first_hbm.at[rows], first_ref.at[rows], first_sem.at[q])
        copy.start()
        first_copies.append(copy)
    turned = taper_ref[...].T
    tapers[:, 0:64] = turned
    tapers[:, 64:128] = turned
    for q in range(4):
        sub_copies[2 * q].wait()
        sub_copies[2 * q + 1].wait()

        @pl.loop(16 * q, 16 * q + 16, unroll=4)
        def _(a):
            rows = pl.ds(pl.multiple_of(a * 128, 128), 128)
            plain[pl.ds(pl.multiple_of(a * PITCH, 8), 128), :] = sub_ref[0, rows, :].astype(f32)
            plain[pl.ds(pl.multiple_of((64 + a) * PITCH, 8), 128), :] = sub_ref[1, rows, :].astype(f32)

    lane = lax.broadcasted_iota(jnp.int32, (1, 128), 1)
    sign = jnp.where(lane < 64, -1.0, 1.0).astype(f32)

    def operands(b):
        data = plain[pl.ds(b, 128, stride=PITCH), :].astype(bf16)
        taper = tapers[pl.ds(b, 1), :]
        table = first_ref[b]
        real = table * taper
        imag = pltpu.roll(table, 64, 1) * (taper * sign)
        high, low = split(jnp.concatenate([real, imag], axis=0))
        return data, jnp.concatenate([high, low], axis=1)

    for q in range(4):
        first_copies[q].wait()

        @pl.loop(16 * q, 16 * q + 16, unroll=16)
        def _(pair):
            data_a, matrix_a = operands(2 * pair)
            data_b, matrix_b = operands(2 * pair + 1)
            data = jnp.concatenate([data_a, data_b], axis=1)
            out = jnp.dot(
                jnp.concatenate([matrix_a, matrix_b], axis=0),
                jnp.concatenate([data, data], axis=0),
                preferred_element_type=f32,
            )
            for j in range(2):
                b = 2 * pair + j
                mine = out[2 * count * j : 2 * count * (j + 1), 128 * j : 128 * j + 128]
                mid[pl.ds(b, count, stride=PITCH_MID), :] = mine[:count]
                mid[pl.ds(128 + b, count, stride=PITCH_MID), :] = mine[count:]

    me = lax.axis_index("facet")
    facets = [(me // 8) * 8 + j for j in range(near)] + [me ^ s for s in subset]
    blocks = [pl.ds(pl.multiple_of(f * 16, 16), 16) for f in facets]
    high = jnp.concatenate([second_ref[rows, 0:256] for rows in blocks], axis=0)
    low = jnp.concatenate([second_ref[rows, 256:512] for rows in blocks], axis=0)
    rows = 16 * number
    if extra:
        row = lax.broadcasted_iota(jnp.int32, (16, 128), 0)
        tile = jnp.where(row == 0, meta_ref[0], jnp.where(row == 1, meta_ref[1], meta_ref[2]))
        tile = tile.astype(f32).astype(bf16)
        for i in range(number):
            pieces[i, count] = tile
    part = count // 2
    for half in range(2):

        @pl.loop(part // 2 * half, part // 2 * (half + 1), unroll=8)
        def _(pair):
            both = []
            for j in range(2):
                start = pl.multiple_of((2 * pair + j) * PITCH_MID, 8)
                both.append(mid[pl.ds(start, 256), :])
            data_high, data_low = split(jnp.concatenate(both, axis=1))
            out = jnp.dot(jnp.concatenate([high, low], axis=0), data_high, preferred_element_type=f32)
            out = out[:rows] + out[rows:] + jnp.dot(high, data_low, preferred_element_type=f32)
            out = out.astype(bf16)
            for i in range(number):
                for j in range(2):
                    pieces[i, 2 * pair + j] = out[i * 16 : i * 16 + 16, j * 128 : j * 128 + 128]

        size = part + (extra if half else 0)
        span = pl.ds(half * part, size)
        if near:
            copy = pltpu.make_async_copy(
                pieces.at[pl.ds(0, near), span], outs[0].at[:, span], out_sem.at[half, len(subset)]
            )
            copy.start()
            out_copies.append(copy)
        for i, start in enumerate(starts):
            if half * part >= start:
                copy = pltpu.make_async_copy(
                    pieces.at[near + i, span],
                    outs[len(outs) - len(subset) + i].at[pl.ds(half * part - start, size)],
                    out_sem.at[half, i],
                )
                copy.start()
                out_copies.append(copy)
    for copy in out_copies:
        copy.wait()


def forward(subgrid, taper, first, second, near, subset, starts, meta=None):
    number, count, extra = near + len(subset), first.shape[1], 0 if meta is None else 1
    shapes = [jax.ShapeDtypeStruct((near, count + extra, 16, 128), bf16)] * (1 if near else 0)
    shapes += [jax.ShapeDtypeStruct((count - start + extra, 16, 128), bf16) for start in starts]
    hbm = pl.BlockSpec(memory_space=pl.ANY)
    return pl.pallas_call(
        functools.partial(
            forward_kernel, near=near, subset=subset, starts=starts, count=count, extra=extra
        ),
        grid=(1,),
        in_specs=[pl.BlockSpec(memory_space=pltpu.SMEM)] * extra
        + [
            hbm,
            pl.BlockSpec((64, 128), lambda i: (0, 0)),
            hbm,
            pl.BlockSpec((256, 512), lambda i: (0, 0)),
        ],
        out_specs=[hbm] * len(shapes),
        out_shape=shapes,
        scratch_shapes=[
            pltpu.VMEM((2, 8192, 128), bf16),
            pltpu.VMEM((128, count, 128), f32),
            pltpu.VMEM((128 * PITCH, 128), f32),
            pltpu.VMEM((128, 128), f32),
            pltpu.VMEM((count * PITCH_MID, 128), f32),
            pltpu.VMEM((number, count + extra, 16, 128), bf16),
            pltpu.SemaphoreType.DMA((4, 2)),
            pltpu.SemaphoreType.DMA((4,)),
            pltpu.SemaphoreType.DMA((2, len(subset) + 1)),
        ],
        compiler_params=pltpu.CompilerParams(vmem_limit_bytes=58 * MIB),
        cost_estimate=pl.CostEstimate(flops=160000000 * count, bytes_accessed=12 * MIB, transcendentals=0),
        name=f"forward{number}",
    )(*([meta] * extra), subgrid, taper, first, second)


def placing_matrix(tiles):
    owner = lax.broadcasted_iota(jnp.int32, (16, 256), 1) >> 4
    meta = jnp.zeros((16, 256), f32)
    for s, tile in enumerate(tiles):
        tile = tile.astype(f32)
        meta = jnp.where(owner == s, jnp.concatenate([tile, tile], axis=1), meta)
    counts, positions, channels = meta[0:1], meta[1:2].astype(jnp.int32), meta[2:3]
    root = jnp.sqrt(counts)
    weight = root * (16.0 / (jnp.sum(root, axis=1, keepdims=True) * (1.0 / 16)))
    half = 0.5 * (CHANNELS - 1)
    level = (channels - half) / half
    row = lax.broadcasted_iota(jnp.int32, (128, 256), 0)
    lane = lax.broadcasted_iota(jnp.int32, (128, 256), 1)
    n1 = positions * 8 + ((lane >> 1) & 7)
    index = (n1 * (row >> 1) + 16 * ((lane & 1) - (row & 1))) & 63
    wave = jnp.cos(index.astype(f32) * (2 * math.pi / 64))
    return jnp.concatenate([wave * weight, wave * (weight * level)], axis=0)


def scale_kernel(correction_ref, table_ref, scaled_ref):
    gains = correction_ref[...].T
    gains = jnp.concatenate([gains, gains], axis=1).T
    for k1 in range(64):
        high, low = split(table_ref[k1] * gains[:, k1 : k1 + 1])
        scaled_ref[k1, :, 0:128] = high
        scaled_ref[k1, :, 128:256] = low


def scale(correction, table):
    whole = lambda shape: pl.BlockSpec(shape, lambda i: (0,) * len(shape))
    shape = jax.ShapeDtypeStruct((64, 128, 256), bf16)
    return pl.pallas_call(
        scale_kernel,
        grid=(1,),
        in_specs=[whole(correction.shape), whole(table.shape)],
        out_specs=whole(shape.shape),
        out_shape=shape,
        compiler_params=pltpu.CompilerParams(vmem_limit_bytes=58 * MIB, dimension_semantics=("arbitrary",)),
        cost_estimate=pl.CostEstimate(flops=6000000000, bytes_accessed=16 * MIB, transcendentals=0),
        name="scale",
    )(correction, table)


def final_kernel(scaled_hbm, *rest, early, far):
    halves, near_ref, wholes = rest[:early], rest[early], rest[early + 1 : early + 1 + far]
    out_hbm, store, held, scaled_ref, image, piece_sem, scaled_sem, out_sem = rest[early + 1 + far :]
    scaled_copies, out_copies = [], []
    piece_copies = [[], [], []]
    near = near_ref.shape[0]

    def fetch(source, target, stage, index):
        copy = pltpu.make_async_copy(source, target, piece_sem.at[stage, index])
        copy.start()
        piece_copies[stage].append(copy)

    for stage, start, size in ((0, 64, 1), (1, 0, 32), (2, 32, 32)):
        span = pl.ds(start, size)
        fetch(near_ref.at[:, span], held.at[pl.ds(0, near), span], stage, far)
        for i, whole in enumerate(wholes):
            if i < early and stage == 1:
                source = halves[i]
            else:
                source = whole.at[pl.ds(start - (32 if i < early else 0), size)]
            fetch(source, held.at[near + i, span], stage, i)
    for q in range(4):
        part = pl.ds(16 * q, 16)
        copy = pltpu.make_async_copy(scaled_hbm.at[part], scaled_ref.at[part], scaled_sem.at[q])
        copy.start()
        scaled_copies.append(copy)
    for copy in piece_copies[0]:
        copy.wait()
    high, low = split(placing_matrix([held[s, 64] for s in range(16)]))
    for half in range(2):
        for copy in piece_copies[1 + half]:
            copy.wait()

        @pl.loop(16 * half, 16 * half + 16, unroll=8)
        def _(pair):
            both = [jnp.concatenate([held[s, 2 * pair + j] for s in range(16)], axis=0) for j in range(2)]
            data = jnp.concatenate(both, axis=1)
            out = jnp.dot(high, data, preferred_element_type=f32) + jnp.dot(low, data, preferred_element_type=f32)
            for j in range(2):
                store[pl.ds(2 * pair + j, 256, stride=PITCH_STAGE), :] = out[:, j * 128 : j * 128 + 128]

    for copy in scaled_copies:
        copy.wait()
    for t in range(2):

        @pl.loop(0, 64, unroll=32)
        def _(k1):
            row = (t * 64 + k1) * (2 * PITCH_STAGE)
            parts = [store[pl.ds(pl.multiple_of(row + x * PITCH_STAGE, 8), 64), :] for x in range(2)]
            data = jnp.concatenate(parts, axis=0).astype(bf16)
            out = jnp.dot(scaled_ref[k1], jnp.concatenate([data, data], axis=0), preferred_element_type=f32)
            for x in range(2):
                start = (t * 2 + x) * (64 * PITCH_IMAGE)
                image[pl.ds(start + k1, 64, stride=PITCH_IMAGE), :] = out[x * 64 : x * 64 + 64]

        for x in range(2):
            source = image.reshape(4, 64, PITCH_IMAGE, 128).at[t * 2 + x, :, pl.ds(0, 64)]
            copy = pltpu.make_async_copy(source, out_hbm.at[t, x], out_sem.at[t, x])
            copy.start()
            out_copies.append(copy)
    for copy in out_copies:
        copy.wait()


def final(scaled, early, near, far):
    hbm = pl.BlockSpec(memory_space=pl.ANY)
    pieces = early + [near] + far
    return pl.pallas_call(
        functools.partial(final_kernel, early=len(early), far=len(far)),
        in_specs=[hbm] * (1 + len(pieces)),
        out_specs=hbm,
        out_shape=jax.ShapeDtypeStruct((2, 2, 64, 64, 128), f32),
        scratch_shapes=[
            pltpu.VMEM((256 * PITCH_STAGE, 128), f32),
            pltpu.VMEM((16, 65, 16, 128), bf16),
            pltpu.VMEM((64, 128, 256), bf16),
            pltpu.VMEM((4 * 64 * PITCH_IMAGE, 128), f32),
            pltpu.SemaphoreType.DMA((3, len(far) + 1)),
            pltpu.SemaphoreType.DMA((4,)),
            pltpu.SemaphoreType.DMA((2, 2)),
        ],
        compiler_params=pltpu.CompilerParams(vmem_limit_bytes=58 * MIB),
        cost_estimate=pl.CostEstimate(flops=8000000000, bytes_accessed=16 * MIB, transcendentals=0),
        name="final",
    )(scaled, *pieces)


NEAR = 8
EARLY = (8, 9, 10, 11)
FAR = (8, 9, 10, 11, 12, 13, 14, 15)


def exchange(piece, s):
    return lax.ppermute(piece, "facet", [(i, i ^ s) for i in range(16)])


def local(subgrids, taper, counts, positions, channels, correction):
    first, second = forward_tables()
    inputs = (subgrids[0], taper.reshape(64, 128))
    early = forward(*inputs, first[:, :32], second, 0, EARLY, (0,) * len(EARLY))
    starts = tuple(32 if s in EARLY else 0 for s in FAR)
    meta = jnp.concatenate([counts, positions, channels])
    near, *far = forward(*inputs, first, second, NEAR, FAR, starts, meta)
    early = [exchange(piece, s) for s, piece in zip(EARLY, early)]
    far = [exchange(piece, s) for s, piece in zip(FAR, far)]
    halves = [list(range(NEAR)), list(range(NEAR, 2 * NEAR))]
    near = lax.all_to_all(near, "facet", split_axis=0, concat_axis=0, axis_index_groups=halves, tiled=True)
    scaled = scale(correction.reshape(64, 64), inverse_table())
    image = final(scaled, early, near, far)
    return image.reshape(TAYLOR, 2, 4096, 128)


def phase_table(height, breadth, length, sign):
    first = jnp.arange(height, dtype=jnp.int32)[:, None]
    second = jnp.arange(breadth, dtype=jnp.int32)[None, :]
    angle = (first * second % length).astype(jnp.float32) * (2.0 * math.pi / length)
    return (jnp.cos(angle), sign * jnp.sin(angle))


def transform(real_part, imag_part, sign):
    length = real_part.shape[-2]
    width = real_part.shape[-1]
    outer = math.gcd(length, 64)
    inner = length // outer
    leading = real_part.shape[:-2]
    real_in = real_part.reshape(leading + (outer, inner, width))
    imag_in = imag_part.reshape(leading + (outer, inner, width))
    high = lax.Precision.HIGHEST
    outer_re, outer_im = phase_table(outer, outer, outer, sign)
    twist_re, twist_im = phase_table(outer, inner, length, sign)
    twist_re = twist_re[:, :, None]
    twist_im = twist_im[:, :, None]
    inner_re, inner_im = phase_table(inner, inner, inner, sign)
    first_re = jnp.einsum("ka,...abr->...kbr", outer_re, real_in, precision=high) - jnp.einsum(
        "ka,...abr->...kbr", outer_im, imag_in, precision=high
    )
    first_im = jnp.einsum("ka,...abr->...kbr", outer_re, imag_in, precision=high) + jnp.einsum(
        "ka,...abr->...kbr", outer_im, real_in, precision=high
    )
    turned_re = first_re * twist_re - first_im * twist_im
    turned_im = first_re * twist_im + first_im * twist_re
    last_re = jnp.einsum("bm,...kbr->...mkr", inner_re, turned_re, precision=high) - jnp.einsum(
        "bm,...kbr->...mkr", inner_im, turned_im, precision=high
    )
    last_im = jnp.einsum("bm,...kbr->...mkr", inner_im, turned_re, precision=high) + jnp.einsum(
        "bm,...kbr->...mkr", inner_re, turned_im, precision=high
    )
    factor = 1.0 / math.sqrt(length)
    return (
        last_re.reshape(leading + (length, width)) * factor,
        last_im.reshape(leading + (length, width)) * factor,
    )


def general(subgrids, taper, counts, positions, channels, correction):
    local_count = subgrids.shape[0]
    facets = lax.axis_size("facet")
    every_count, every_position, every_channel = (
        lax.all_gather(counts, "facet", axis=0, tiled=True),
        lax.all_gather(positions, "facet", axis=0, tiled=True),
        lax.all_gather(channels, "facet", axis=0, tiled=True),
    )
    data = subgrids[0].astype(jnp.float32) * taper[:, None]
    wave_re, wave_im = transform(data[0], data[1], -1.0)
    block = jnp.stack([wave_re, wave_im]).astype(jnp.bfloat16)[None]
    received_list = [lax.all_to_all(block, "facet", split_axis=2, concat_axis=0, tiled=True)]
    stacked = jnp.stack(received_list, axis=1)
    received = stacked.reshape((facets * local_count,) + stacked.shape[2:])
    root = jnp.sqrt(every_count.astype(jnp.float32))
    weight = root * (root.shape[0] / jnp.sum(root))
    half = 0.5 * (CHANNELS - 1)
    level = (every_channel.astype(jnp.float32) - half) / half
    terms = [weight]
    terms.append(terms[-1] * level)
    taylor = jnp.stack(terms)
    contrib = received.shape[2]
    rows = received.shape[3]
    slot_count = correction.shape[0] // contrib
    slots = (every_position[None, :] == jnp.arange(slot_count, dtype=jnp.int32)[:, None]).astype(
        jnp.float32
    )
    table = taylor[:, None, :] * slots[None]
    buffer = jnp.einsum(
        "tqs,sxcr->txqcr", table, received.astype(jnp.float32), precision=lax.Precision.HIGHEST
    )
    buffer = buffer.reshape(TAYLOR, 2, slot_count * contrib, rows)
    field_re, field_im = transform(buffer[:, 0], buffer[:, 1], 1.0)
    return jnp.stack([field_re, field_im], axis=1) * correction[:, None]


def solution(mesh):
    placed = (
        P(("grp", "facet"), None, None, None),
        P(),
        P(("grp", "facet")),
        P(("grp", "facet")),
        P(("grp", "facet")),
        P("facet"),
    )
    own = local if mesh.shape["facet"] == 16 else general
    return jax.shard_map(
        own, mesh=mesh, in_specs=placed, out_specs=P(None, None, "facet", "grp"), check_vma=False
    )
```

```python
import functools
import math

import jax
import jax.numpy as jnp
import numpy as np
from jax import lax
from jax.experimental import pallas as pl
from jax.experimental.pallas import tpu as pltpu
from jax.sharding import PartitionSpec as P

TAYLOR = 2
CHANNELS = 96
MIB = 1024 * 1024
f32 = jnp.float32
bf16 = jnp.bfloat16

PITCH, PITCH_MID, PITCH_STAGE, PITCH_IMAGE = 136, 264, 72, 72


def split(value):
    high = value.astype(bf16)
    return high, (value - high.astype(f32)).astype(bf16)


def forward_tables():
    b = np.arange(128)[:, None, None]
    ka = np.arange(64)[None, :, None]
    a = np.arange(64)[None, None, :]
    angle = 2 * np.pi * (((128 * a + b) * ka) % 8192) / 8192.0
    first = np.concatenate([np.cos(angle), np.sin(angle)], axis=2).astype(np.float32)
    kb = np.arange(128)[:, None]
    angle = 2 * np.pi * ((kb * kb.T) % 128) / 128
    cos = (np.cos(angle) / math.sqrt(8192.0)).reshape(16, 8, 128)
    sin = (np.sin(angle) / math.sqrt(8192.0)).reshape(16, 8, 128)
    second = np.empty((16, 8, 2, 2, 128))
    second[:, :, 0, 0], second[:, :, 0, 1] = cos, sin
    second[:, :, 1, 0], second[:, :, 1, 1] = -sin, cos
    second = second.reshape(256, 256).astype(np.float32)
    high = second.astype(bf16)
    low = (second - high.astype(np.float32)).astype(bf16)
    return first, np.concatenate([high, low], axis=1)


def inverse_table():
    k1 = np.arange(64)[:, None, None]
    k2 = np.arange(64)[None, :, None]
    cell = np.arange(64)[None, None, :]
    angle = 2 * np.pi * ((cell * (k1 + 64 * k2)) % 4096) / 4096.0
    cos, sin = np.cos(angle) / 64.0, np.sin(angle) / 64.0
    table = np.empty((64, 2, 64, 2, 64), np.float32)
    table[:, 0, :, 0], table[:, 0, :, 1] = cos, -sin
    table[:, 1, :, 0], table[:, 1, :, 1] = sin, cos
    return table.reshape(64, 128, 128)


def forward_kernel(*rest, near, subset, starts, count, extra):
    if extra:
        meta_ref, _, *rest = rest
    sub_hbm, taper_ref, first_hbm, second_ref, *rest = rest
    number = near + len(subset)
    outs = rest[: len(subset) + (1 if near else 0)]
    sub_ref, first_ref, plain, tapers, mid, pieces, sub_sem, first_sem, out_sem = rest[len(outs) :]
    sub_copies, first_copies, out_copies = [], [], []
    for q in range(4):
        for x in range(2):
            rows = pl.ds(q * 2048, 2048)
            copy = pltpu.make_async_copy(sub_hbm.at[x, rows], sub_ref.at[x, rows], sub_sem.at[q, x])
            copy.start()
            sub_copies.append(copy)
    for q in range(4):
        rows = pl.ds(q * 32, 32)
        copy = pltpu.make_async_copy(first_hbm.at[rows], first_ref.at[rows], first_sem.at[q])
        copy.start()
        first_copies.append(copy)
    turned = taper_ref[...].T
    tapers[:, 0:64] = turned
    tapers[:, 64:128] = turned
    for q in range(4):
        sub_copies[2 * q].wait()
        sub_copies[2 * q + 1].wait()

        @pl.loop(16 * q, 16 * q + 16, unroll=4)
        def _(a):
            rows = pl.ds(pl.multiple_of(a * 128, 128), 128)
            plain[pl.ds(pl.multiple_of(a * PITCH, 8), 128), :] = sub_ref[0, rows, :].astype(f32)
            plain[pl.ds(pl.multiple_of((64 + a) * PITCH, 8), 128), :] = sub_ref[1, rows, :].astype(f32)

    lane = lax.broadcasted_iota(jnp.int32, (1, 128), 1)
    sign = jnp.where(lane < 64, -1.0, 1.0).astype(f32)

    def operands(b):
        data = plain[pl.ds(b, 128, stride=PITCH), :].astype(bf16)
        taper = tapers[pl.ds(b, 1), :]
        table = first_ref[b]
        real = table * taper
        imag = pltpu.roll(table, 64, 1) * (taper * sign)
        high, low = split(jnp.concatenate([real, imag], axis=0))
        return data, jnp.concatenate([high, low], axis=1)

    for q in range(4):
        first_copies[q].wait()

        @pl.loop(16 * q, 16 * q + 16, unroll=16)
        def _(pair):
            data_a, matrix_a = operands(2 * pair)
            data_b, matrix_b = operands(2 * pair + 1)
            data = jnp.concatenate([data_a, data_b], axis=1)
            out = jnp.dot(
                jnp.concatenate([matrix_a, matrix_b], axis=0),
                jnp.concatenate([data, data], axis=0),
                preferred_element_type=f32,
            )
            for j in range(2):
                b = 2 * pair + j
                mine = out[2 * count * j : 2 * count * (j + 1), 128 * j : 128 * j + 128]
                mid[pl.ds(b, count, stride=PITCH_MID), :] = mine[:count]
                mid[pl.ds(128 + b, count, stride=PITCH_MID), :] = mine[count:]

    me = lax.axis_index("facet")
    facets = [(me // 8) * 8 + j for j in range(near)] + [me ^ s for s in subset]
    blocks = [pl.ds(pl.multiple_of(f * 16, 16), 16) for f in facets]
    high = jnp.concatenate([second_ref[rows, 0:256] for rows in blocks], axis=0)
    low = jnp.concatenate([second_ref[rows, 256:512] for rows in blocks], axis=0)
    rows = 16 * number
    if extra:
        row = lax.broadcasted_iota(jnp.int32, (16, 128), 0)
        tile = jnp.where(row == 0, meta_ref[0], jnp.where(row == 1, meta_ref[1], meta_ref[2]))
        tile = tile.astype(f32).astype(bf16)
        for i in range(number):
            pieces[i, count] = tile
    part = count // 2
    for half in range(2):

        @pl.loop(part // 2 * half, part // 2 * (half + 1), unroll=8)
        def _(pair):
            both = []
            for j in range(2):
                start = pl.multiple_of((2 * pair + j) * PITCH_MID, 8)
                both.append(mid[pl.ds(start, 256), :])
            data_high, data_low = split(jnp.concatenate(both, axis=1))
            out = jnp.dot(jnp.concatenate([high, low], axis=0), data_high, preferred_element_type=f32)
            out = out[:rows] + out[rows:] + jnp.dot(high, data_low, preferred_element_type=f32)
            out = out.astype(bf16)
            for i in range(number):
                for j in range(2):
                    pieces[i, 2 * pair + j] = out[i * 16 : i * 16 + 16, j * 128 : j * 128 + 128]

        size = part + (extra if half else 0)
        span = pl.ds(half * part, size)
        if near:
            copy = pltpu.make_async_copy(
                pieces.at[pl.ds(0, near), span], outs[0].at[:, span], out_sem.at[half, len(subset)]
            )
            copy.start()
            out_copies.append(copy)
        for i, start in enumerate(starts):
            if half * part >= start:
                copy = pltpu.make_async_copy(
                    pieces.at[near + i, span],
                    outs[len(outs) - len(subset) + i].at[pl.ds(half * part - start, size)],
                    out_sem.at[half, i],
                )
                copy.start()
                out_copies.append(copy)
    for copy in out_copies:
        copy.wait()


def forward(subgrid, taper, first, second, near, subset, starts, meta=None, after=None):
    number, count, extra = near + len(subset), first.shape[1], 0 if meta is None else 1
    shapes = [jax.ShapeDtypeStruct((near, count + extra, 16, 128), bf16)] * (1 if near else 0)
    shapes += [jax.ShapeDtypeStruct((count - start + extra, 16, 128), bf16) for start in starts]
    hbm = pl.BlockSpec(memory_space=pl.ANY)
    return pl.pallas_call(
        functools.partial(
            forward_kernel, near=near, subset=subset, starts=starts, count=count, extra=extra
        ),
        grid=(1,),
        in_specs=[pl.BlockSpec(memory_space=pltpu.SMEM), hbm][: 2 * extra]
        + [
            hbm,
            pl.BlockSpec((64, 128), lambda i: (0, 0)),
            hbm,
            pl.BlockSpec((256, 512), lambda i: (0, 0)),
        ],
        out_specs=[hbm] * len(shapes),
        out_shape=shapes,
        scratch_shapes=[
            pltpu.VMEM((2, 8192, 128), bf16),
            pltpu.VMEM((128, count, 128), f32),
            pltpu.VMEM((128 * PITCH, 128), f32),
            pltpu.VMEM((128, 128), f32),
            pltpu.VMEM((count * PITCH_MID, 128), f32),
            pltpu.VMEM((number, count + extra, 16, 128), bf16),
            pltpu.SemaphoreType.DMA((4, 2)),
            pltpu.SemaphoreType.DMA((4,)),
            pltpu.SemaphoreType.DMA((2, len(subset) + 1)),
        ],
        compiler_params=pltpu.CompilerParams(vmem_limit_bytes=58 * MIB),
        cost_estimate=pl.CostEstimate(flops=160000000 * count, bytes_accessed=12 * MIB, transcendentals=0),
        name=f"forward{number}",
    )(*([meta, after] if extra else []), subgrid, taper, first, second)


def placing_matrix(tiles):
    owner = lax.broadcasted_iota(jnp.int32, (16, 256), 1) >> 4
    meta = jnp.zeros((16, 256), f32)
    for s, tile in enumerate(tiles):
        tile = tile.astype(f32)
        meta = jnp.where(owner == s, jnp.concatenate([tile, tile], axis=1), meta)
    counts, positions, channels = meta[0:1], meta[1:2].astype(jnp.int32), meta[2:3]
    root = jnp.sqrt(counts)
    weight = root * (16.0 / (jnp.sum(root, axis=1, keepdims=True) * (1.0 / 16)))
    half = 0.5 * (CHANNELS - 1)
    level = (channels - half) / half
    row = lax.broadcasted_iota(jnp.int32, (128, 256), 0)
    lane = lax.broadcasted_iota(jnp.int32, (128, 256), 1)
    n1 = positions * 8 + ((lane >> 1) & 7)
    index = (n1 * (row >> 1) + 16 * ((lane & 1) - (row & 1))) & 63
    wave = jnp.cos(index.astype(f32) * (2 * math.pi / 64))
    return jnp.concatenate([wave * weight, wave * (weight * level)], axis=0)


def scale_kernel(correction_ref, table_ref, scaled_ref):
    gains = correction_ref[...].T
    gains = jnp.concatenate([gains, gains], axis=1).T
    for k1 in range(64):
        high, low = split(table_ref[k1] * gains[:, k1 : k1 + 1])
        scaled_ref[k1, :, 0:128] = high
        scaled_ref[k1, :, 128:256] = low


def scale(correction, table):
    whole = lambda shape: pl.BlockSpec(shape, lambda i: (0,) * len(shape))
    shape = jax.ShapeDtypeStruct((64, 128, 256), bf16)
    return pl.pallas_call(
        scale_kernel,
        grid=(1,),
        in_specs=[whole(correction.shape), whole(table.shape)],
        out_specs=whole(shape.shape),
        out_shape=shape,
        compiler_params=pltpu.CompilerParams(vmem_limit_bytes=24 * MIB, dimension_semantics=("arbitrary",)),
        cost_estimate=pl.CostEstimate(flops=6000000000, bytes_accessed=16 * MIB, transcendentals=0),
        name="scale",
    )(correction, table)


def final_kernel(scaled_hbm, *rest, early, far):
    halves, near_ref, wholes = rest[:early], rest[early], rest[early + 1 : early + 1 + far]
    out_hbm, store, held, scaled_ref, image, piece_sem, scaled_sem, out_sem = rest[early + 1 + far :]
    scaled_copies, out_copies = [], []
    piece_copies = [[], [], []]
    near = near_ref.shape[0]

    def fetch(source, target, stage, index):
        copy = pltpu.make_async_copy(source, target, piece_sem.at[stage, index])
        copy.start()
        piece_copies[stage].append(copy)

    for stage, start, size in ((0, 64, 1), (1, 0, 32), (2, 32, 32)):
        span = pl.ds(start, size)
        fetch(near_ref.at[:, span], held.at[pl.ds(0, near), span], stage, far)
        for i, whole in enumerate(wholes):
            if i < early and stage == 1:
                source = halves[i]
            else:
                source = whole.at[pl.ds(start - (32 if i < early else 0), size)]
            fetch(source, held.at[near + i, span], stage, i)
    for q in range(4):
        part = pl.ds(16 * q, 16)
        copy = pltpu.make_async_copy(scaled_hbm.at[part], scaled_ref.at[part], scaled_sem.at[q])
        copy.start()
        scaled_copies.append(copy)
    for copy in piece_copies[0]:
        copy.wait()
    high, low = split(placing_matrix([held[s, 64] for s in range(16)]))
    for half in range(2):
        for copy in piece_copies[1 + half]:
            copy.wait()

        @pl.loop(16 * half, 16 * half + 16, unroll=8)
        def _(pair):
            both = [jnp.concatenate([held[s, 2 * pair + j] for s in range(16)], axis=0) for j in range(2)]
            data = jnp.concatenate(both, axis=1)
            out = jnp.dot(high, data, preferred_element_type=f32) + jnp.dot(low, data, preferred_element_type=f32)
            for j in range(2):
                store[pl.ds(2 * pair + j, 256, stride=PITCH_STAGE), :] = out[:, j * 128 : j * 128 + 128]

    for copy in scaled_copies:
        copy.wait()
    for t in range(2):

        @pl.loop(0, 64, unroll=32)
        def _(k1):
            row = (t * 64 + k1) * (2 * PITCH_STAGE)
            parts = [store[pl.ds(pl.multiple_of(row + x * PITCH_STAGE, 8), 64), :] for x in range(2)]
            data = jnp.concatenate(parts, axis=0).astype(bf16)
            out = jnp.dot(scaled_ref[k1], jnp.concatenate([data, data], axis=0), preferred_element_type=f32)
            for x in range(2):
                start = (t * 2 + x) * (64 * PITCH_IMAGE)
                image[pl.ds(start + k1, 64, stride=PITCH_IMAGE), :] = out[x * 64 : x * 64 + 64]

        for x in range(2):
            source = image.reshape(4, 64, PITCH_IMAGE, 128).at[t * 2 + x, :, pl.ds(0, 64)]
            copy = pltpu.make_async_copy(source, out_hbm.at[t, x], out_sem.at[t, x])
            copy.start()
            out_copies.append(copy)
    for copy in out_copies:
        copy.wait()


def final(scaled, early, near, far):
    hbm = pl.BlockSpec(memory_space=pl.ANY)
    pieces = early + [near] + far
    return pl.pallas_call(
        functools.partial(final_kernel, early=len(early), far=len(far)),
        in_specs=[hbm] * (1 + len(pieces)),
        out_specs=hbm,
        out_shape=jax.ShapeDtypeStruct((2, 2, 64, 64, 128), f32),
        scratch_shapes=[
            pltpu.VMEM((256 * PITCH_STAGE, 128), f32),
            pltpu.VMEM((16, 65, 16, 128), bf16),
            pltpu.VMEM((64, 128, 256), bf16),
            pltpu.VMEM((4 * 64 * PITCH_IMAGE, 128), f32),
            pltpu.SemaphoreType.DMA((3, len(far) + 1)),
            pltpu.SemaphoreType.DMA((4,)),
            pltpu.SemaphoreType.DMA((2, 2)),
        ],
        compiler_params=pltpu.CompilerParams(vmem_limit_bytes=34 * MIB),
        cost_estimate=pl.CostEstimate(flops=8000000000, bytes_accessed=16 * MIB, transcendentals=0),
        name="final",
    )(scaled, *pieces)


NEAR = 8
EARLY = (8, 9, 10, 11)
FAR = (8, 9, 10, 11, 12, 13, 14, 15)


def exchange(piece, s):
    return lax.ppermute(piece, "facet", [(i, i ^ s) for i in range(16)])


def local(subgrids, taper, counts, positions, channels, correction):
    first, second = forward_tables()
    inputs = (subgrids[0], taper.reshape(64, 128))
    early = forward(*inputs, first[:, :32], second, 0, EARLY, (0,) * len(EARLY))
    starts = tuple(32 if s in EARLY else 0 for s in FAR)
    meta = jnp.concatenate([counts, positions, channels])
    near, *far = forward(*inputs, first, second, NEAR, FAR, starts, meta, early[-1])
    early = [exchange(piece, s) for s, piece in zip(EARLY, early)]
    far = [exchange(piece, s) for s, piece in zip(FAR, far)]
    halves = [list(range(NEAR)), list(range(NEAR, 2 * NEAR))]
    near = lax.all_to_all(near, "facet", split_axis=0, concat_axis=0, axis_index_groups=halves, tiled=True)
    scaled = scale(correction.reshape(64, 64), inverse_table())
    image = final(scaled, early, near, far)
    return image.reshape(TAYLOR, 2, 4096, 128)


def phase_table(height, breadth, length, sign):
    first = jnp.arange(height, dtype=jnp.int32)[:, None]
    second = jnp.arange(breadth, dtype=jnp.int32)[None, :]
    angle = (first * second % length).astype(jnp.float32) * (2.0 * math.pi / length)
    return (jnp.cos(angle), sign * jnp.sin(angle))


def transform(real_part, imag_part, sign):
    length = real_part.shape[-2]
    width = real_part.shape[-1]
    outer = math.gcd(length, 64)
    inner = length // outer
    leading = real_part.shape[:-2]
    real_in = real_part.reshape(leading + (outer, inner, width))
    imag_in = imag_part.reshape(leading + (outer, inner, width))
    high = lax.Precision.HIGHEST
    outer_re, outer_im = phase_table(outer, outer, outer, sign)
    twist_re, twist_im = phase_table(outer, inner, length, sign)
    twist_re = twist_re[:, :, None]
    twist_im = twist_im[:, :, None]
    inner_re, inner_im = phase_table(inner, inner, inner, sign)
    first_re = jnp.einsum("ka,...abr->...kbr", outer_re, real_in, precision=high) - jnp.einsum(
        "ka,...abr->...kbr", outer_im, imag_in, precision=high
    )
    first_im = jnp.einsum("ka,...abr->...kbr", outer_re, imag_in, precision=high) + jnp.einsum(
        "ka,...abr->...kbr", outer_im, real_in, precision=high
    )
    turned_re = first_re * twist_re - first_im * twist_im
    turned_im = first_re * twist_im + first_im * twist_re
    last_re = jnp.einsum("bm,...kbr->...mkr", inner_re, turned_re, precision=high) - jnp.einsum(
        "bm,...kbr->...mkr", inner_im, turned_im, precision=high
    )
    last_im = jnp.einsum("bm,...kbr->...mkr", inner_im, turned_re, precision=high) + jnp.einsum(
        "bm,...kbr->...mkr", inner_re, turned_im, precision=high
    )
    factor = 1.0 / math.sqrt(length)
    return (
        last_re.reshape(leading + (length, width)) * factor,
        last_im.reshape(leading + (length, width)) * factor,
    )


def general(subgrids, taper, counts, positions, channels, correction):
    local_count = subgrids.shape[0]
    facets = lax.axis_size("facet")
    every_count, every_position, every_channel = (
        lax.all_gather(counts, "facet", axis=0, tiled=True),
        lax.all_gather(positions, "facet", axis=0, tiled=True),
        lax.all_gather(channels, "facet", axis=0, tiled=True),
    )
    data = subgrids[0].astype(jnp.float32) * taper[:, None]
    wave_re, wave_im = transform(data[0], data[1], -1.0)
    block = jnp.stack([wave_re, wave_im]).astype(jnp.bfloat16)[None]
    received_list = [lax.all_to_all(block, "facet", split_axis=2, concat_axis=0, tiled=True)]
    stacked = jnp.stack(received_list, axis=1)
    received = stacked.reshape((facets * local_count,) + stacked.shape[2:])
    root = jnp.sqrt(every_count.astype(jnp.float32))
    weight = root * (root.shape[0] / jnp.sum(root))
    half = 0.5 * (CHANNELS - 1)
    level = (every_channel.astype(jnp.float32) - half) / half
    terms = [weight]
    terms.append(terms[-1] * level)
    taylor = jnp.stack(terms)
    contrib = received.shape[2]
    rows = received.shape[3]
    slot_count = correction.shape[0] // contrib
    slots = (every_position[None, :] == jnp.arange(slot_count, dtype=jnp.int32)[:, None]).astype(
        jnp.float32
    )
    table = taylor[:, None, :] * slots[None]
    buffer = jnp.einsum(
        "tqs,sxcr->txqcr", table, received.astype(jnp.float32), precision=lax.Precision.HIGHEST
    )
    buffer = buffer.reshape(TAYLOR, 2, slot_count * contrib, rows)
    field_re, field_im = transform(buffer[:, 0], buffer[:, 1], 1.0)
    return jnp.stack([field_re, field_im], axis=1) * correction[:, None]


def solution(mesh):
    placed = (
        P(("grp", "facet"), None, None, None),
        P(),
        P(("grp", "facet")),
        P(("grp", "facet")),
        P(("grp", "facet")),
        P("facet"),
    )
    own = local if mesh.shape["facet"] == 16 else general
    return jax.shard_map(
        own, mesh=mesh, in_specs=placed, out_specs=P(None, None, "facet", "grp"), check_vma=False
    )
```

```python
import functools
import math

import jax
import jax.numpy as jnp
import numpy as np
from jax import lax
from jax.experimental import pallas as pl
from jax.experimental.pallas import tpu as pltpu
from jax.sharding import PartitionSpec as P

TAYLOR = 2
CHANNELS = 96
MIB = 1024 * 1024
f32 = jnp.float32
bf16 = jnp.bfloat16

PITCH, PITCH_MID, PITCH_STAGE, PITCH_IMAGE = 136, 264, 72, 72


def split(value):
    high = value.astype(bf16)
    return high, (value - high.astype(f32)).astype(bf16)


def forward_tables():
    b = np.arange(128)[:, None, None]
    ka = np.arange(64)[None, :, None]
    a = np.arange(64)[None, None, :]
    angle = 2 * np.pi * (((128 * a + b) * ka) % 8192) / 8192.0
    first = np.concatenate([np.cos(angle), np.sin(angle)], axis=2).astype(np.float32)
    kb = np.arange(128)[:, None]
    angle = 2 * np.pi * ((kb * kb.T) % 128) / 128
    cos = (np.cos(angle) / math.sqrt(8192.0)).reshape(16, 8, 128)
    sin = (np.sin(angle) / math.sqrt(8192.0)).reshape(16, 8, 128)
    second = np.empty((16, 8, 2, 2, 128))
    second[:, :, 0, 0], second[:, :, 0, 1] = cos, sin
    second[:, :, 1, 0], second[:, :, 1, 1] = -sin, cos
    second = second.reshape(256, 256).astype(np.float32)
    high = second.astype(bf16)
    low = (second - high.astype(np.float32)).astype(bf16)
    return first, np.concatenate([high, low], axis=1)


def inverse_table():
    k1 = np.arange(64)[:, None, None]
    k2 = np.arange(64)[None, :, None]
    cell = np.arange(64)[None, None, :]
    angle = 2 * np.pi * ((cell * (k1 + 64 * k2)) % 4096) / 4096.0
    cos, sin = np.cos(angle) / 64.0, np.sin(angle) / 64.0
    table = np.empty((64, 2, 64, 2, 64), np.float32)
    table[:, 0, :, 0], table[:, 0, :, 1] = cos, -sin
    table[:, 1, :, 0], table[:, 1, :, 1] = sin, cos
    return table.reshape(64, 128, 128)


def forward_kernel(*rest, subset, starts, count, extra):
    if extra:
        meta_ref, *rest = rest
    sub_hbm, taper_ref, first_hbm, second_ref, *rest = rest
    outs = rest[: len(subset)]
    sub_ref, first_ref, plain, tapers, mid, pieces, sub_sem, first_sem, out_sem = rest[len(subset) :]
    sub_copies, first_copies, out_copies = [], [], []
    for q in range(4):
        for x in range(2):
            rows = pl.ds(q * 2048, 2048)
            copy = pltpu.make_async_copy(sub_hbm.at[x, rows], sub_ref.at[x, rows], sub_sem.at[q, x])
            copy.start()
            sub_copies.append(copy)
    for q in range(4):
        rows = pl.ds(q * 32, 32)
        copy = pltpu.make_async_copy(first_hbm.at[rows], first_ref.at[rows], first_sem.at[q])
        copy.start()
        first_copies.append(copy)
    turned = taper_ref[...].T
    tapers[:, 0:64] = turned
    tapers[:, 64:128] = turned
    for q in range(4):
        sub_copies[2 * q].wait()
        sub_copies[2 * q + 1].wait()

        @pl.loop(16 * q, 16 * q + 16, unroll=4)
        def _(a):
            rows = pl.ds(pl.multiple_of(a * 128, 128), 128)
            plain[pl.ds(pl.multiple_of(a * PITCH, 8), 128), :] = sub_ref[0, rows, :].astype(f32)
            plain[pl.ds(pl.multiple_of((64 + a) * PITCH, 8), 128), :] = sub_ref[1, rows, :].astype(f32)

    lane = lax.broadcasted_iota(jnp.int32, (1, 128), 1)
    sign = jnp.where(lane < 64, -1.0, 1.0).astype(f32)

    def operands(b):
        data = plain[pl.ds(b, 128, stride=PITCH), :].astype(bf16)
        taper = tapers[pl.ds(b, 1), :]
        table = first_ref[b]
        real = table * taper
        imag = pltpu.roll(table, 64, 1) * (taper * sign)
        high, low = split(jnp.concatenate([real, imag], axis=0))
        return data, jnp.concatenate([high, low], axis=1)

    for q in range(4):
        first_copies[q].wait()

        @pl.loop(16 * q, 16 * q + 16, unroll=16)
        def _(pair):
            data_a, matrix_a = operands(2 * pair)
            data_b, matrix_b = operands(2 * pair + 1)
            data = jnp.concatenate([data_a, data_b], axis=1)
            out = jnp.dot(
                jnp.concatenate([matrix_a, matrix_b], axis=0),
                jnp.concatenate([data, data], axis=0),
                preferred_element_type=f32,
            )
            for j in range(2):
                b = 2 * pair + j
                mine = out[2 * count * j : 2 * count * (j + 1), 128 * j : 128 * j + 128]
                mid[pl.ds(b, count, stride=PITCH_MID), :] = mine[:count]
                mid[pl.ds(128 + b, count, stride=PITCH_MID), :] = mine[count:]

    me = lax.axis_index("facet")
    blocks = [pl.ds(pl.multiple_of((me ^ s) * 16, 16), 16) for s in subset]
    high = jnp.concatenate([second_ref[rows, 0:256] for rows in blocks], axis=0)
    low = jnp.concatenate([second_ref[rows, 256:512] for rows in blocks], axis=0)
    rows = 16 * len(subset)
    if extra:
        row = lax.broadcasted_iota(jnp.int32, (16, 128), 0)
        tile = jnp.where(row == 0, meta_ref[0], jnp.where(row == 1, meta_ref[1], meta_ref[2]))
        tile = tile.astype(f32).astype(bf16)
        for i in range(len(subset)):
            pieces[i, count] = tile
    part = count // 2
    for half in range(2):

        @pl.loop(part // 2 * half, part // 2 * (half + 1), unroll=8)
        def _(pair):
            both = []
            for j in range(2):
                start = pl.multiple_of((2 * pair + j) * PITCH_MID, 8)
                both.append(mid[pl.ds(start, 256), :])
            data_high, data_low = split(jnp.concatenate(both, axis=1))
            out = jnp.dot(jnp.concatenate([high, low], axis=0), data_high, preferred_element_type=f32)
            out = out[:rows] + out[rows:] + jnp.dot(high, data_low, preferred_element_type=f32)
            out = out.astype(bf16)
            for i in range(len(subset)):
                for j in range(2):
                    pieces[i, 2 * pair + j] = out[i * 16 : i * 16 + 16, j * 128 : j * 128 + 128]

        size = part + (extra if half else 0)
        for i, start in enumerate(starts):
            if half * part >= start:
                copy = pltpu.make_async_copy(
                    pieces.at[i, pl.ds(half * part, size)],
                    outs[i].at[pl.ds(half * part - start, size)],
                    out_sem.at[half, i],
                )
                copy.start()
                out_copies.append(copy)
    for copy in out_copies:
        copy.wait()


def forward(subgrid, taper, first, second, subset, starts, meta=None):
    number, count, extra = len(subset), first.shape[1], 0 if meta is None else 1
    shapes = [jax.ShapeDtypeStruct((count - start + extra, 16, 128), bf16) for start in starts]
    hbm = pl.BlockSpec(memory_space=pl.ANY)
    return pl.pallas_call(
        functools.partial(forward_kernel, subset=subset, starts=starts, count=count, extra=extra),
        grid=(1,),
        in_specs=[pl.BlockSpec(memory_space=pltpu.SMEM)] * extra
        + [
            hbm,
            pl.BlockSpec((64, 128), lambda i: (0, 0)),
            hbm,
            pl.BlockSpec((256, 512), lambda i: (0, 0)),
        ],
        out_specs=[hbm] * number,
        out_shape=shapes,
        scratch_shapes=[
            pltpu.VMEM((2, 8192, 128), bf16),
            pltpu.VMEM((128, count, 128), f32),
            pltpu.VMEM((128 * PITCH, 128), f32),
            pltpu.VMEM((128, 128), f32),
            pltpu.VMEM((count * PITCH_MID, 128), f32),
            pltpu.VMEM((number, count + extra, 16, 128), bf16),
            pltpu.SemaphoreType.DMA((4, 2)),
            pltpu.SemaphoreType.DMA((4,)),
            pltpu.SemaphoreType.DMA((2, number)),
        ],
        compiler_params=pltpu.CompilerParams(vmem_limit_bytes=58 * MIB),
        cost_estimate=pl.CostEstimate(flops=160000000 * count, bytes_accessed=12 * MIB, transcendentals=0),
        name=f"forward{number}",
    )(*([meta] * extra), subgrid, taper, first, second)


def placing_matrix(tiles):
    owner = lax.broadcasted_iota(jnp.int32, (16, 256), 1) >> 4
    meta = jnp.zeros((16, 256), f32)
    for s, tile in enumerate(tiles):
        tile = tile.astype(f32)
        meta = jnp.where(owner == s, jnp.concatenate([tile, tile], axis=1), meta)
    counts, positions, channels = meta[0:1], meta[1:2].astype(jnp.int32), meta[2:3]
    root = jnp.sqrt(counts)
    weight = root * (16.0 / (jnp.sum(root, axis=1, keepdims=True) * (1.0 / 16)))
    half = 0.5 * (CHANNELS - 1)
    level = (channels - half) / half
    row = lax.broadcasted_iota(jnp.int32, (128, 256), 0)
    lane = lax.broadcasted_iota(jnp.int32, (128, 256), 1)
    n1 = positions * 8 + ((lane >> 1) & 7)
    index = (n1 * (row >> 1) + 16 * ((lane & 1) - (row & 1))) & 63
    wave = jnp.cos(index.astype(f32) * (2 * math.pi / 64))
    return jnp.concatenate([wave * weight, wave * (weight * level)], axis=0)


def scale_kernel(correction_ref, table_ref, scaled_ref):
    gains = correction_ref[...].T
    gains = jnp.concatenate([gains, gains], axis=1).T
    for k1 in range(64):
        high, low = split(table_ref[k1] * gains[:, k1 : k1 + 1])
        scaled_ref[k1, :, 0:128] = high
        scaled_ref[k1, :, 128:256] = low


def scale(correction, table):
    whole = lambda shape: pl.BlockSpec(shape, lambda i: (0,) * len(shape))
    shape = jax.ShapeDtypeStruct((64, 128, 256), bf16)
    return pl.pallas_call(
        scale_kernel,
        grid=(1,),
        in_specs=[whole(correction.shape), whole(table.shape)],
        out_specs=whole(shape.shape),
        out_shape=shape,
        compiler_params=pltpu.CompilerParams(vmem_limit_bytes=58 * MIB, dimension_semantics=("arbitrary",)),
        cost_estimate=pl.CostEstimate(flops=6000000000, bytes_accessed=16 * MIB, transcendentals=0),
        name="scale",
    )(correction, table)


def final_kernel(scaled_hbm, *rest, sizes):
    refs = rest[: len(sizes)]
    out_hbm, store, held, scaled_ref, image, piece_sem, scaled_sem, out_sem = rest[len(sizes) :]
    scaled_copies, out_copies = [], []
    piece_copies = [[], [], []]

    def fetch(ref, at, s, stage, start, size):
        target = held.at[s, pl.ds(start, size)]
        copy = pltpu.make_async_copy(ref.at[pl.ds(at, size)], target, piece_sem.at[stage, s])
        copy.start()
        piece_copies[stage].append(copy)

    wholes = refs[len(sizes) - 16 :]
    halves = refs[: len(sizes) - 16]
    for s, ref in enumerate(wholes):
        fetch(ref, ref.shape[0] - 1, s, 0, 64, 1)
    for s, ref in enumerate(wholes):
        fetch(halves[s] if s < len(halves) else ref, 0, s, 1, 0, 32)
    for s, ref in enumerate(wholes):
        fetch(ref, 0 if s < len(halves) else 32, s, 2, 32, 32)
    for q in range(4):
        part = pl.ds(16 * q, 16)
        copy = pltpu.make_async_copy(scaled_hbm.at[part], scaled_ref.at[part], scaled_sem.at[q])
        copy.start()
        scaled_copies.append(copy)
    for copy in piece_copies[0]:
        copy.wait()
    high, low = split(placing_matrix([held[s, 64] for s in range(16)]))
    for half in range(2):
        for copy in piece_copies[1 + half]:
            copy.wait()

        @pl.loop(16 * half, 16 * half + 16, unroll=8)
        def _(pair):
            both = [jnp.concatenate([held[s, 2 * pair + j] for s in range(16)], axis=0) for j in range(2)]
            data = jnp.concatenate(both, axis=1)
            out = jnp.dot(high, data, preferred_element_type=f32) + jnp.dot(low, data, preferred_element_type=f32)
            for j in range(2):
                store[pl.ds(2 * pair + j, 256, stride=PITCH_STAGE), :] = out[:, j * 128 : j * 128 + 128]

    for copy in scaled_copies:
        copy.wait()
    for t in range(2):

        @pl.loop(0, 64, unroll=32)
        def _(k1):
            row = (t * 64 + k1) * (2 * PITCH_STAGE)
            parts = [store[pl.ds(pl.multiple_of(row + x * PITCH_STAGE, 8), 64), :] for x in range(2)]
            data = jnp.concatenate(parts, axis=0).astype(bf16)
            out = jnp.dot(scaled_ref[k1], jnp.concatenate([data, data], axis=0), preferred_element_type=f32)
            for x in range(2):
                start = (t * 2 + x) * (64 * PITCH_IMAGE)
                image[pl.ds(start + k1, 64, stride=PITCH_IMAGE), :] = out[x * 64 : x * 64 + 64]

        for x in range(2):
            source = image.reshape(4, 64, PITCH_IMAGE, 128).at[t * 2 + x, :, pl.ds(0, 64)]
            copy = pltpu.make_async_copy(source, out_hbm.at[t, x], out_sem.at[t, x])
            copy.start()
            out_copies.append(copy)
    for copy in out_copies:
        copy.wait()


def final(scaled, pieces):
    hbm = pl.BlockSpec(memory_space=pl.ANY)
    sizes = tuple(piece.shape[0] for piece in pieces)
    return pl.pallas_call(
        functools.partial(final_kernel, sizes=sizes),
        in_specs=[hbm] * (1 + len(pieces)),
        out_specs=hbm,
        out_shape=jax.ShapeDtypeStruct((2, 2, 64, 64, 128), f32),
        scratch_shapes=[
            pltpu.VMEM((256 * PITCH_STAGE, 128), f32),
            pltpu.VMEM((16, 65, 16, 128), bf16),
            pltpu.VMEM((64, 128, 256), bf16),
            pltpu.VMEM((4 * 64 * PITCH_IMAGE, 128), f32),
            pltpu.SemaphoreType.DMA((3, 16)),
            pltpu.SemaphoreType.DMA((4,)),
            pltpu.SemaphoreType.DMA((2, 2)),
        ],
        compiler_params=pltpu.CompilerParams(vmem_limit_bytes=58 * MIB),
        cost_estimate=pl.CostEstimate(flops=8000000000, bytes_accessed=16 * MIB, transcendentals=0),
        name="final",
    )(scaled, *pieces)


EARLY = (8, 9, 10, 11)
LATE = (8, 9, 10, 11, 4, 12, 3, 5, 13, 2, 6, 14, 7, 15, 1)


def exchange(piece, s):
    return lax.ppermute(piece, "facet", [(i, i ^ s) for i in range(16)])


def local(subgrids, taper, counts, positions, channels, correction):
    first, second = forward_tables()
    inputs = (subgrids[0], taper.reshape(64, 128))
    early = forward(*inputs, first[:, :32], second, EARLY, (0,) * len(EARLY))
    starts = tuple(32 if s in EARLY else 0 for s in LATE) + (0,)
    meta = jnp.concatenate([counts, positions, channels])
    late = forward(*inputs, first, second, LATE + (0,), starts, meta)
    early = [exchange(piece, s) for s, piece in zip(EARLY, early)]
    late = [exchange(piece, s) for s, piece in zip(LATE, late)] + [late[15]]
    scaled = scale(correction.reshape(64, 64), inverse_table())
    image = final(scaled, early + late)
    return image.reshape(TAYLOR, 2, 4096, 128)


def phase_table(height, breadth, length, sign):
    first = jnp.arange(height, dtype=jnp.int32)[:, None]
    second = jnp.arange(breadth, dtype=jnp.int32)[None, :]
    angle = (first * second % length).astype(jnp.float32) * (2.0 * math.pi / length)
    return (jnp.cos(angle), sign * jnp.sin(angle))


def transform(real_part, imag_part, sign):
    length = real_part.shape[-2]
    width = real_part.shape[-1]
    outer = math.gcd(length, 64)
    inner = length // outer
    leading = real_part.shape[:-2]
    real_in = real_part.reshape(leading + (outer, inner, width))
    imag_in = imag_part.reshape(leading + (outer, inner, width))
    high = lax.Precision.HIGHEST
    outer_re, outer_im = phase_table(outer, outer, outer, sign)
    twist_re, twist_im = phase_table(outer, inner, length, sign)
    twist_re = twist_re[:, :, None]
    twist_im = twist_im[:, :, None]
    inner_re, inner_im = phase_table(inner, inner, inner, sign)
    first_re = jnp.einsum("ka,...abr->...kbr", outer_re, real_in, precision=high) - jnp.einsum(
        "ka,...abr->...kbr", outer_im, imag_in, precision=high
    )
    first_im = jnp.einsum("ka,...abr->...kbr", outer_re, imag_in, precision=high) + jnp.einsum(
        "ka,...abr->...kbr", outer_im, real_in, precision=high
    )
    turned_re = first_re * twist_re - first_im * twist_im
    turned_im = first_re * twist_im + first_im * twist_re
    last_re = jnp.einsum("bm,...kbr->...mkr", inner_re, turned_re, precision=high) - jnp.einsum(
        "bm,...kbr->...mkr", inner_im, turned_im, precision=high
    )
    last_im = jnp.einsum("bm,...kbr->...mkr", inner_im, turned_re, precision=high) + jnp.einsum(
        "bm,...kbr->...mkr", inner_re, turned_im, precision=high
    )
    factor = 1.0 / math.sqrt(length)
    return (
        last_re.reshape(leading + (length, width)) * factor,
        last_im.reshape(leading + (length, width)) * factor,
    )


def general(subgrids, taper, counts, positions, channels, correction):
    local_count = subgrids.shape[0]
    facets = lax.axis_size("facet")
    every_count, every_position, every_channel = (
        lax.all_gather(counts, "facet", axis=0, tiled=True),
        lax.all_gather(positions, "facet", axis=0, tiled=True),
        lax.all_gather(channels, "facet", axis=0, tiled=True),
    )
    data = subgrids[0].astype(jnp.float32) * taper[:, None]
    wave_re, wave_im = transform(data[0], data[1], -1.0)
    block = jnp.stack([wave_re, wave_im]).astype(jnp.bfloat16)[None]
    received_list = [lax.all_to_all(block, "facet", split_axis=2, concat_axis=0, tiled=True)]
    stacked = jnp.stack(received_list, axis=1)
    received = stacked.reshape((facets * local_count,) + stacked.shape[2:])
    root = jnp.sqrt(every_count.astype(jnp.float32))
    weight = root * (root.shape[0] / jnp.sum(root))
    half = 0.5 * (CHANNELS - 1)
    level = (every_channel.astype(jnp.float32) - half) / half
    terms = [weight]
    terms.append(terms[-1] * level)
    taylor = jnp.stack(terms)
    contrib = received.shape[2]
    rows = received.shape[3]
    slot_count = correction.shape[0] // contrib
    slots = (every_position[None, :] == jnp.arange(slot_count, dtype=jnp.int32)[:, None]).astype(
        jnp.float32
    )
    table = taylor[:, None, :] * slots[None]
    buffer = jnp.einsum(
        "tqs,sxcr->txqcr", table, received.astype(jnp.float32), precision=lax.Precision.HIGHEST
    )
    buffer = buffer.reshape(TAYLOR, 2, slot_count * contrib, rows)
    field_re, field_im = transform(buffer[:, 0], buffer[:, 1], 1.0)
    return jnp.stack([field_re, field_im], axis=1) * correction[:, None]


def solution(mesh):
    placed = (
        P(("grp", "facet"), None, None, None),
        P(),
        P(("grp", "facet")),
        P(("grp", "facet")),
        P(("grp", "facet")),
        P("facet"),
    )
    own = local if mesh.shape["facet"] == 16 else general
    return jax.shard_map(
        own, mesh=mesh, in_specs=placed, out_specs=P(None, None, "facet", "grp"), check_vma=False
    )
```

```python
import functools
import math

import jax
import jax.numpy as jnp
import numpy as np
from jax import lax
from jax.experimental import pallas as pl
from jax.experimental.pallas import tpu as pltpu
from jax.sharding import PartitionSpec as P

TAYLOR = 2
CHANNELS = 96
MIB = 1024 * 1024
f32 = jnp.float32
bf16 = jnp.bfloat16

PITCH, PITCH_MID, PITCH_STAGE, PITCH_IMAGE = 136, 264, 72, 72


def split(value):
    high = value.astype(bf16)
    return high, (value - high.astype(f32)).astype(bf16)


def forward_tables():
    b = np.arange(128)[:, None, None]
    ka = np.arange(64)[None, :, None]
    a = np.arange(64)[None, None, :]
    angle = 2 * np.pi * (((128 * a + b) * ka) % 8192) / 8192.0
    first = np.concatenate([np.cos(angle), np.sin(angle)], axis=2).astype(np.float32)
    kb = np.arange(128)[:, None]
    angle = 2 * np.pi * ((kb * kb.T) % 128) / 128
    cos = (np.cos(angle) / math.sqrt(8192.0)).reshape(16, 8, 128)
    sin = (np.sin(angle) / math.sqrt(8192.0)).reshape(16, 8, 128)
    second = np.empty((16, 8, 2, 2, 128))
    second[:, :, 0, 0], second[:, :, 0, 1] = cos, sin
    second[:, :, 1, 0], second[:, :, 1, 1] = -sin, cos
    second = second.reshape(256, 256).astype(np.float32)
    high = second.astype(bf16)
    low = (second - high.astype(np.float32)).astype(bf16)
    return first, np.concatenate([high, low], axis=1)


def inverse_table():
    k1 = np.arange(64)[:, None, None]
    k2 = np.arange(64)[None, :, None]
    cell = np.arange(64)[None, None, :]
    angle = 2 * np.pi * ((cell * (k1 + 64 * k2)) % 4096) / 4096.0
    cos, sin = np.cos(angle) / 64.0, np.sin(angle) / 64.0
    table = np.empty((64, 2, 64, 2, 64), np.float32)
    table[:, 0, :, 0], table[:, 0, :, 1] = cos, -sin
    table[:, 1, :, 0], table[:, 1, :, 1] = sin, cos
    return table.reshape(64, 128, 128)


def forward_kernel(*rest, subset, starts, count, extra):
    if extra:
        meta_ref, *rest = rest
    sub_hbm, taper_hbm, first_hbm, second_hbm, *rest = rest
    outs = rest[: len(subset)]
    sub_ref, taper_ref, first_ref, second_ref, plain, tapers, mid, pieces, sub_sem, first_sem, out_sem = rest[len(subset) :]
    sub_copies, first_copies, out_copies = [], [], []
    taper_copy = pltpu.make_async_copy(taper_hbm, taper_ref, first_sem.at[4])
    taper_copy.start()
    for q in range(4):
        for x in range(2):
            rows = pl.ds(q * 2048, 2048)
            copy = pltpu.make_async_copy(sub_hbm.at[x, rows], sub_ref.at[x, rows], sub_sem.at[q, x])
            copy.start()
            sub_copies.append(copy)
    for q in range(4):
        rows = pl.ds(q * 32, 32)
        copy = pltpu.make_async_copy(first_hbm.at[rows], first_ref.at[rows], first_sem.at[q])
        copy.start()
        first_copies.append(copy)
    second_copy = pltpu.make_async_copy(second_hbm, second_ref, first_sem.at[5])
    second_copy.start()
    taper_copy.wait()
    turned = taper_ref[...].T
    tapers[:, 0:64] = turned
    tapers[:, 64:128] = turned
    for q in range(4):
        sub_copies[2 * q].wait()
        sub_copies[2 * q + 1].wait()

        @pl.loop(16 * q, 16 * q + 16, unroll=4)
        def _(a):
            rows = pl.ds(pl.multiple_of(a * 128, 128), 128)
            plain[pl.ds(pl.multiple_of(a * PITCH, 8), 128), :] = sub_ref[0, rows, :].astype(f32)
            plain[pl.ds(pl.multiple_of((64 + a) * PITCH, 8), 128), :] = sub_ref[1, rows, :].astype(f32)

    lane = lax.broadcasted_iota(jnp.int32, (1, 128), 1)
    sign = jnp.where(lane < 64, -1.0, 1.0).astype(f32)

    def operands(b):
        data = plain[pl.ds(b, 128, stride=PITCH), :].astype(bf16)
        taper = tapers[pl.ds(b, 1), :]
        table = first_ref[b]
        real = table * taper
        imag = pltpu.roll(table, 64, 1) * (taper * sign)
        high, low = split(jnp.concatenate([real, imag], axis=0))
        return data, jnp.concatenate([high, low], axis=1)

    for q in range(4):
        first_copies[q].wait()

        @pl.loop(16 * q, 16 * q + 16, unroll=16)
        def _(pair):
            data_a, matrix_a = operands(2 * pair)
            data_b, matrix_b = operands(2 * pair + 1)
            data = jnp.concatenate([data_a, data_b], axis=1)
            out = jnp.dot(
                jnp.concatenate([matrix_a, matrix_b], axis=0),
                jnp.concatenate([data, data], axis=0),
                preferred_element_type=f32,
            )
            for j in range(2):
                b = 2 * pair + j
                mine = out[2 * count * j : 2 * count * (j + 1), 128 * j : 128 * j + 128]
                mid[pl.ds(b, count, stride=PITCH_MID), :] = mine[:count]
                mid[pl.ds(128 + b, count, stride=PITCH_MID), :] = mine[count:]

    second_copy.wait()
    me = lax.axis_index("facet")
    blocks = [pl.ds(pl.multiple_of((me ^ s) * 16, 16), 16) for s in subset]
    high = jnp.concatenate([second_ref[rows, 0:256] for rows in blocks], axis=0)
    low = jnp.concatenate([second_ref[rows, 256:512] for rows in blocks], axis=0)
    rows = 16 * len(subset)
    if extra:
        row = lax.broadcasted_iota(jnp.int32, (16, 128), 0)
        tile = jnp.where(row == 0, meta_ref[0], jnp.where(row == 1, meta_ref[1], meta_ref[2]))
        tile = tile.astype(f32).astype(bf16)
        for i in range(len(subset)):
            pieces[i, count] = tile
    part = count // 2
    for half in range(2):

        @pl.loop(part // 2 * half, part // 2 * (half + 1), unroll=8)
        def _(pair):
            both = []
            for j in range(2):
                start = pl.multiple_of((2 * pair + j) * PITCH_MID, 8)
                both.append(mid[pl.ds(start, 256), :])
            data_high, data_low = split(jnp.concatenate(both, axis=1))
            out = jnp.dot(jnp.concatenate([high, low], axis=0), data_high, preferred_element_type=f32)
            out = out[:rows] + out[rows:] + jnp.dot(high, data_low, preferred_element_type=f32)
            out = out.astype(bf16)
            for i in range(len(subset)):
                for j in range(2):
                    pieces[i, 2 * pair + j] = out[i * 16 : i * 16 + 16, j * 128 : j * 128 + 128]

        size = part + (extra if half else 0)
        for i, start in enumerate(starts):
            if half * part >= start:
                copy = pltpu.make_async_copy(
                    pieces.at[i, pl.ds(half * part, size)],
                    outs[i].at[pl.ds(half * part - start, size)],
                    out_sem.at[half, i],
                )
                copy.start()
                out_copies.append(copy)
    for copy in out_copies:
        copy.wait()


def forward(subgrid, taper, first, second, subset, starts, meta=None):
    number, count, extra = len(subset), first.shape[1], 0 if meta is None else 1
    shapes = [jax.ShapeDtypeStruct((count - start + extra, 16, 128), bf16) for start in starts]
    hbm = pl.BlockSpec(memory_space=pl.ANY)
    return pl.pallas_call(
        functools.partial(forward_kernel, subset=subset, starts=starts, count=count, extra=extra),
        grid=(1,),
        in_specs=[pl.BlockSpec(memory_space=pltpu.SMEM)] * extra
        + [
            hbm,
            hbm,
            hbm,
            hbm,
        ],
        out_specs=[hbm] * number,
        out_shape=shapes,
        scratch_shapes=[
            pltpu.VMEM((2, 8192, 128), bf16),
            pltpu.VMEM((64, 128), f32),
            pltpu.VMEM((128, count, 128), f32),
            pltpu.VMEM((256, 512), bf16),
            pltpu.VMEM((128 * PITCH, 128), f32),
            pltpu.VMEM((128, 128), f32),
            pltpu.VMEM((count * PITCH_MID, 128), f32),
            pltpu.VMEM((number, count + extra, 16, 128), bf16),
            pltpu.SemaphoreType.DMA((4, 2)),
            pltpu.SemaphoreType.DMA((6,)),
            pltpu.SemaphoreType.DMA((2, number)),
        ],
        compiler_params=pltpu.CompilerParams(vmem_limit_bytes=58 * MIB),
        cost_estimate=pl.CostEstimate(flops=160000000 * count, bytes_accessed=12 * MIB, transcendentals=0),
        name=f"forward{number}",
    )(*([meta] * extra), subgrid, taper, first, second)


def placing_matrix(tiles):
    owner = lax.broadcasted_iota(jnp.int32, (16, 256), 1) >> 4
    meta = jnp.zeros((16, 256), f32)
    for s, tile in enumerate(tiles):
        tile = tile.astype(f32)
        meta = jnp.where(owner == s, jnp.concatenate([tile, tile], axis=1), meta)
    counts, positions, channels = meta[0:1], meta[1:2].astype(jnp.int32), meta[2:3]
    root = jnp.sqrt(counts)
    weight = root * (16.0 / (jnp.sum(root, axis=1, keepdims=True) * (1.0 / 16)))
    half = 0.5 * (CHANNELS - 1)
    level = (channels - half) / half
    row = lax.broadcasted_iota(jnp.int32, (128, 256), 0)
    lane = lax.broadcasted_iota(jnp.int32, (128, 256), 1)
    n1 = positions * 8 + ((lane >> 1) & 7)
    index = (n1 * (row >> 1) + 16 * ((lane & 1) - (row & 1))) & 63
    wave = jnp.cos(index.astype(f32) * (2 * math.pi / 64))
    return jnp.concatenate([wave * weight, wave * (weight * level)], axis=0)


def scale_kernel(correction_ref, table_ref, scaled_ref):
    gains = correction_ref[...].T
    gains = jnp.concatenate([gains, gains], axis=1).T
    for k1 in range(64):
        high, low = split(table_ref[k1] * gains[:, k1 : k1 + 1])
        scaled_ref[k1, :, 0:128] = high
        scaled_ref[k1, :, 128:256] = low


def scale(correction, table):
    whole = lambda shape: pl.BlockSpec(shape, lambda i: (0,) * len(shape))
    shape = jax.ShapeDtypeStruct((64, 128, 256), bf16)
    return pl.pallas_call(
        scale_kernel,
        grid=(1,),
        in_specs=[whole(correction.shape), whole(table.shape)],
        out_specs=whole(shape.shape),
        out_shape=shape,
        compiler_params=pltpu.CompilerParams(vmem_limit_bytes=58 * MIB, dimension_semantics=("arbitrary",)),
        cost_estimate=pl.CostEstimate(flops=6000000000, bytes_accessed=16 * MIB, transcendentals=0),
        name="scale",
    )(correction, table)


def final_kernel(scaled_hbm, *rest, sizes):
    refs = rest[: len(sizes)]
    out_hbm, store, held, scaled_ref, image, piece_sem, scaled_sem, out_sem = rest[len(sizes) :]
    scaled_copies, out_copies = [], []
    piece_copies = [[], [], []]

    def fetch(ref, at, s, stage, start, size):
        target = held.at[s, pl.ds(start, size)]
        copy = pltpu.make_async_copy(ref.at[pl.ds(at, size)], target, piece_sem.at[stage, s])
        copy.start()
        piece_copies[stage].append(copy)

    wholes = refs[len(sizes) - 16 :]
    halves = refs[: len(sizes) - 16]
    for s, ref in enumerate(wholes):
        fetch(ref, ref.shape[0] - 1, s, 0, 64, 1)
    for s, ref in enumerate(wholes):
        fetch(halves[s] if s < len(halves) else ref, 0, s, 1, 0, 32)
    for s, ref in enumerate(wholes):
        fetch(ref, 0 if s < len(halves) else 32, s, 2, 32, 32)
    for q in range(4):
        part = pl.ds(16 * q, 16)
        copy = pltpu.make_async_copy(scaled_hbm.at[part], scaled_ref.at[part], scaled_sem.at[q])
        copy.start()
        scaled_copies.append(copy)
    for copy in piece_copies[0]:
        copy.wait()
    high, low = split(placing_matrix([held[s, 64] for s in range(16)]))
    for half in range(2):
        for copy in piece_copies[1 + half]:
            copy.wait()

        @pl.loop(16 * half, 16 * half + 16, unroll=8)
        def _(pair):
            both = [jnp.concatenate([held[s, 2 * pair + j] for s in range(16)], axis=0) for j in range(2)]
            data = jnp.concatenate(both, axis=1)
            out = jnp.dot(high, data, preferred_element_type=f32) + jnp.dot(low, data, preferred_element_type=f32)
            for j in range(2):
                store[pl.ds(2 * pair + j, 256, stride=PITCH_STAGE), :] = out[:, j * 128 : j * 128 + 128]

    for copy in scaled_copies:
        copy.wait()
    for t in range(2):

        @pl.loop(0, 64, unroll=32)
        def _(k1):
            row = (t * 64 + k1) * (2 * PITCH_STAGE)
            parts = [store[pl.ds(pl.multiple_of(row + x * PITCH_STAGE, 8), 64), :] for x in range(2)]
            data = jnp.concatenate(parts, axis=0).astype(bf16)
            out = jnp.dot(scaled_ref[k1], jnp.concatenate([data, data], axis=0), preferred_element_type=f32)
            for x in range(2):
                start = (t * 2 + x) * (64 * PITCH_IMAGE)
                image[pl.ds(start + k1, 64, stride=PITCH_IMAGE), :] = out[x * 64 : x * 64 + 64]

        for x in range(2):
            source = image.reshape(4, 64, PITCH_IMAGE, 128).at[t * 2 + x, :, pl.ds(0, 64)]
            copy = pltpu.make_async_copy(source, out_hbm.at[t, x], out_sem.at[t, x])
            copy.start()
            out_copies.append(copy)
    for copy in out_copies:
        copy.wait()


def final(scaled, pieces):
    hbm = pl.BlockSpec(memory_space=pl.ANY)
    sizes = tuple(piece.shape[0] for piece in pieces)
    return pl.pallas_call(
        functools.partial(final_kernel, sizes=sizes),
        in_specs=[hbm] * (1 + len(pieces)),
        out_specs=hbm,
        out_shape=jax.ShapeDtypeStruct((2, 2, 64, 64, 128), f32),
        scratch_shapes=[
            pltpu.VMEM((256 * PITCH_STAGE, 128), f32),
            pltpu.VMEM((16, 65, 16, 128), bf16),
            pltpu.VMEM((64, 128, 256), bf16),
            pltpu.VMEM((4 * 64 * PITCH_IMAGE, 128), f32),
            pltpu.SemaphoreType.DMA((3, 16)),
            pltpu.SemaphoreType.DMA((4,)),
            pltpu.SemaphoreType.DMA((2, 2)),
        ],
        compiler_params=pltpu.CompilerParams(vmem_limit_bytes=58 * MIB),
        cost_estimate=pl.CostEstimate(flops=8000000000, bytes_accessed=16 * MIB, transcendentals=0),
        name="final",
    )(scaled, *pieces)


EARLY = (8, 9, 10, 11)
LATE = (8, 9, 10, 11, 4, 12, 3, 5, 13, 2, 6, 14, 7, 15, 1)


def exchange(piece, s):
    return lax.ppermute(piece, "facet", [(i, i ^ s) for i in range(16)])


def local(subgrids, taper, counts, positions, channels, correction):
    first, second = forward_tables()
    inputs = (subgrids[0], taper.reshape(64, 128))
    early = forward(*inputs, first[:, :32], second, EARLY, (0,) * len(EARLY))
    starts = tuple(32 if s in EARLY else 0 for s in LATE) + (0,)
    meta = jnp.concatenate([counts, positions, channels])
    late = forward(*inputs, first, second, LATE + (0,), starts, meta)
    early = [exchange(piece, s) for s, piece in zip(EARLY, early)]
    late = [exchange(piece, s) for s, piece in zip(LATE, late)] + [late[15]]
    scaled = scale(correction.reshape(64, 64), inverse_table())
    image = final(scaled, early + late)
    return image.reshape(TAYLOR, 2, 4096, 128)


def phase_table(height, breadth, length, sign):
    first = jnp.arange(height, dtype=jnp.int32)[:, None]
    second = jnp.arange(breadth, dtype=jnp.int32)[None, :]
    angle = (first * second % length).astype(jnp.float32) * (2.0 * math.pi / length)
    return (jnp.cos(angle), sign * jnp.sin(angle))


def transform(real_part, imag_part, sign):
    length = real_part.shape[-2]
    width = real_part.shape[-1]
    outer = math.gcd(length, 64)
    inner = length // outer
    leading = real_part.shape[:-2]
    real_in = real_part.reshape(leading + (outer, inner, width))
    imag_in = imag_part.reshape(leading + (outer, inner, width))
    high = lax.Precision.HIGHEST
    outer_re, outer_im = phase_table(outer, outer, outer, sign)
    twist_re, twist_im = phase_table(outer, inner, length, sign)
    twist_re = twist_re[:, :, None]
    twist_im = twist_im[:, :, None]
    inner_re, inner_im = phase_table(inner, inner, inner, sign)
    first_re = jnp.einsum("ka,...abr->...kbr", outer_re, real_in, precision=high) - jnp.einsum(
        "ka,...abr->...kbr", outer_im, imag_in, precision=high
    )
    first_im = jnp.einsum("ka,...abr->...kbr", outer_re, imag_in, precision=high) + jnp.einsum(
        "ka,...abr->...kbr", outer_im, real_in, precision=high
    )
    turned_re = first_re * twist_re - first_im * twist_im
    turned_im = first_re * twist_im + first_im * twist_re
    last_re = jnp.einsum("bm,...kbr->...mkr", inner_re, turned_re, precision=high) - jnp.einsum(
        "bm,...kbr->...mkr", inner_im, turned_im, precision=high
    )
    last_im = jnp.einsum("bm,...kbr->...mkr", inner_im, turned_re, precision=high) + jnp.einsum(
        "bm,...kbr->...mkr", inner_re, turned_im, precision=high
    )
    factor = 1.0 / math.sqrt(length)
    return (
        last_re.reshape(leading + (length, width)) * factor,
        last_im.reshape(leading + (length, width)) * factor,
    )


def general(subgrids, taper, counts, positions, channels, correction):
    local_count = subgrids.shape[0]
    facets = lax.axis_size("facet")
    every_count, every_position, every_channel = (
        lax.all_gather(counts, "facet", axis=0, tiled=True),
        lax.all_gather(positions, "facet", axis=0, tiled=True),
        lax.all_gather(channels, "facet", axis=0, tiled=True),
    )
    data = subgrids[0].astype(jnp.float32) * taper[:, None]
    wave_re, wave_im = transform(data[0], data[1], -1.0)
    block = jnp.stack([wave_re, wave_im]).astype(jnp.bfloat16)[None]
    received_list = [lax.all_to_all(block, "facet", split_axis=2, concat_axis=0, tiled=True)]
    stacked = jnp.stack(received_list, axis=1)
    received = stacked.reshape((facets * local_count,) + stacked.shape[2:])
    root = jnp.sqrt(every_count.astype(jnp.float32))
    weight = root * (root.shape[0] / jnp.sum(root))
    half = 0.5 * (CHANNELS - 1)
    level = (every_channel.astype(jnp.float32) - half) / half
    terms = [weight]
    terms.append(terms[-1] * level)
    taylor = jnp.stack(terms)
    contrib = received.shape[2]
    rows = received.shape[3]
    slot_count = correction.shape[0] // contrib
    slots = (every_position[None, :] == jnp.arange(slot_count, dtype=jnp.int32)[:, None]).astype(
        jnp.float32
    )
    table = taylor[:, None, :] * slots[None]
    buffer = jnp.einsum(
        "tqs,sxcr->txqcr", table, received.astype(jnp.float32), precision=lax.Precision.HIGHEST
    )
    buffer = buffer.reshape(TAYLOR, 2, slot_count * contrib, rows)
    field_re, field_im = transform(buffer[:, 0], buffer[:, 1], 1.0)
    return jnp.stack([field_re, field_im], axis=1) * correction[:, None]


def solution(mesh):
    placed = (
        P(("grp", "facet"), None, None, None),
        P(),
        P(("grp", "facet")),
        P(("grp", "facet")),
        P(("grp", "facet")),
        P("facet"),
    )
    own = local if mesh.shape["facet"] == 16 else general
    return jax.shard_map(
        own, mesh=mesh, in_specs=placed, out_specs=P(None, None, "facet", "grp"), check_vma=False
    )
```
